256 devices in a mesh: dom: 64 (over x, z, core), rep: 4 (over y).
Axes of the slice: x: 4, y: 4, z: 8, core: 2. Of those that a mesh axis runs over, the one named last changes fastest.
Arguments:
- elem_rows: bfloat16 [524288, 512], P(('dom', 'rep')), may hold values from -6 to 6
- elem_block: int32 [524288], P(('dom', 'rep')), may hold values from 0 to 3
- send_lists: int32 [524288], P(('dom', 'rep')), may hold values from 0 to 2047, as said below
- halo_block: int32 [524288], P(('dom', 'rep')), may hold values from 0 to 3
- born_rows: bfloat16 [131072, 512], P(('dom', 'rep')), may hold values from -6 to 6
- born_owner: int32 [131072, 1], P(('dom', 'rep')), may hold values from 0 to 255; in each aligned block of 512 rows (0 to 511, 512 to 1023, ...) at most 4 rows name the same one
- mass: float32 [131072], P(('dom', 'rep')), may hold values from 0.5 to 4
Outputs:
- factor: float32 [131072, 512], P(('dom', 'rep'))
The draws below stay inside these ranges and needn't reach their ends.
Inputs may be any that keep to these rules, and one draw needn't show every extreme that they name: `send_lists`: each half of one device's list names 1024 distinct rows of that device. `born_owner`: among the born rows of one device at most 4 name the same owner.
All inputs are finite; a program needn't handle non-finite values.
Results may differ from the reference program's by a relative error of at most 0.0003.
Values may be sent and summed in bfloat16 or wider, within the bound.
No kernel may reach another device: no remote copies, remote signals or barrier semaphores. Data moves between devices by JAX's collectives and lax.ppermute only.
A program may use at most 64 MiB of HBM per device.

```python
import math
import jax
import jax.numpy as jnp
import numpy as np
from jax import lax

W = 512
E_DEV = 2048
H = 1024
CAP = 4
NBLK = 256
BORN_DEV = 512
N_DOM = 64
N_REP = 4


def draw_send_lists(key, part):
    device_keys = jax.random.split(jax.random.fold_in(key, 17), NBLK * 2)

    def one_half(half_key):
        return jax.random.permutation(half_key, E_DEV)[:H]
    chosen = jax.vmap(one_half)(device_keys)
    return chosen.reshape(-1).astype(jnp.int32)


def touch_ends(values, key, smallest, high):
    longest = values.shape.index(max(values.shape))
    spots = []
    for shift in (0, 1):
        where = [jax.random.randint(jax.random.fold_in(key, axis), (), 0, length) for axis, length in enumerate(values.shape)]
        where[longest] = (where[longest] + shift) % values.shape[longest]
        spots.append(tuple(where))
    return values.at[spots[0]].set(smallest).at[spots[1]].set(high)


def block_scale(key, dims, cuts, low, top_value):
    level = 1.0
    for dim, blocks in cuts:
        heights = jax.random.uniform(jax.random.fold_in(jax.random.fold_in(key, 6), dim), (blocks,), jnp.float32, low / len(cuts), top_value / len(cuts))
        level = level * jnp.repeat(jnp.exp(heights), dims[dim] // blocks).reshape((-1,) + (1,) * (len(dims) - 1 - dim))
    return level


def assign_block(key, own, number, rows, amount, top, bound, skew):
    ranking = jax.random.permutation(key, amount)
    packed, common = portions_of(amount, rows * top, bound, skew, True), portions_of(amount, rows * top, bound, skew, False)
    places = jnp.arange(amount)

    def named(tallies, offset_by):
        used = int((tallies > 0).sum())
        fixed = max(1, used // 4)
        passed = fixed + (places - fixed + offset_by * (used - fixed)) % max(1, amount - fixed)
        return jnp.zeros((amount,), jnp.int32).at[ranking[jnp.where(places < fixed, places, passed)]].set(jnp.asarray(tallies, jnp.int32))

    tallies = jnp.where(number % 4 == 0, named(packed, number // 4), named(common, number - number // 4 - 1))
    mixed = jax.random.permutation(jax.random.fold_in(own, 3), amount)
    donor, taker = mixed[0:amount // 2 * 2:2], mixed[1:amount // 2 * 2:2]
    room = jnp.minimum(tallies[donor] - 1, bound - tallies[taker]) // 2
    room = jnp.where((donor == ranking[0]) | (taker == ranking[0]) | (tallies[taker] == 0), 0, jnp.maximum(room, 0))
    passed = jax.random.randint(jax.random.fold_in(own, 4), (amount // 2,), 0, 1 << 20) % (room + 1)
    tallies = tallies.at[donor].add(-passed).at[taker].add(passed)
    members = jnp.searchsorted(jnp.cumsum(tallies), jnp.arange(rows * top), side="right").astype(jnp.int32)
    table = members.reshape(top, rows).T
    table = table[jax.random.permutation(jax.random.fold_in(own, 1), rows)]
    offset_by = jax.random.randint(jax.random.fold_in(own, 2), (rows, 1), 0, top)
    return jnp.take_along_axis(table, (jnp.arange(top)[None, :] + offset_by) % top, axis=1)


def portions_of(number_of, total, bound, slope, full):
    weights = [(1 << 20) // math.isqrt(rank ** slope) + 1 for rank in range(1, number_of + 1)]
    largest = bound if full else min(bound, max(-(-total // number_of), total * weights[0] // sum(weights)))
    least = 1 if total - largest >= number_of - 1 else 0
    holding, spare = [largest] + [least] * (number_of - 1), total - largest - least * (number_of - 1)
    while spare > 0:
        free = [i for i in range(1, number_of) if holding[i] < largest] or [i for i in range(1, number_of) if holding[i] < bound]
        pool, left = sum([weights[i] for i in free]), spare
        for i in free:
            extra = min(bound - holding[i], max(1, left * weights[i] // pool), spare)
            holding[i] = holding[i] + extra
            spare = spare - extra
    return np.array(holding)


def normal_values(key, shape, deviation, limit, cuts=(), held_as=jnp.bfloat16):
    result = jax.random.normal(key, shape, jnp.float32) * deviation
    if len(cuts) > 0:
        result = block_scale(key, shape, cuts, -0.22, 0.18) * result
    return jnp.clip(result, min=-limit, max=limit).astype(held_as)


def setup_inputs(seed: int = 0) -> dict:
    streams_of = jax.random.split(jax.random.key(seed), 8)
    elem_rows = normal_values(streams_of[0], (NBLK * E_DEV, W), 1.0, 6.0, ((0, 256),))
    elem_block = touch_ends(jax.random.randint(streams_of[1], (NBLK * E_DEV,), 0, N_REP), jax.random.fold_in(streams_of[1], 1), 0, N_REP - 1).astype(jnp.int32)
    send_lists = draw_send_lists(jax.random.fold_in(streams_of[7], 71), 0)
    halo_block = touch_ends(jax.random.randint(streams_of[3], (NBLK * 2 * H,), 0, N_REP), jax.random.fold_in(streams_of[3], 1), 0, N_REP - 1).astype(jnp.int32)
    born_rows = normal_values(streams_of[4], (NBLK * BORN_DEV, W), 1.0, 6.0, ((0, 256),))
    born_owner_keys = jax.random.split(jax.random.fold_in(streams_of[5], 1), (NBLK * BORN_DEV) // BORN_DEV)
    born_owner_turns = jax.random.permutation(jax.random.fold_in(streams_of[5], 3), (NBLK * BORN_DEV) // BORN_DEV)
    born_owner = jax.vmap(lambda own, number: assign_block(jax.random.fold_in(streams_of[5], 2), own, number, BORN_DEV, NBLK, 1, CAP, 2))(born_owner_keys, born_owner_turns).reshape((NBLK * BORN_DEV, 1))
    mass = jnp.clip(0.5 + 3.5 * jax.random.uniform(streams_of[6], (NBLK * W,), jnp.float32) ** block_scale(streams_of[6], (NBLK * W,), ((0, 256),), -0.2, 0.2), 0.5, 4.0)
    return {"elem_rows": elem_rows, "elem_block": elem_block, "send_lists": send_lists, "halo_block": halo_block, "born_rows": born_rows, "born_owner": born_owner, "mass": mass}


def pick_rows(row_data, chosen):
    return jnp.take(row_data, chosen, axis=0)

def reference(elem_rows, elem_block, send_lists, halo_block, born_rows, born_owner, mass):
    rows_dev = elem_rows.reshape(NBLK, E_DEV, W)
    list_pairs = send_lists.reshape(NBLK, 2 * H)
    listed_rows = jax.vmap(pick_rows)(rows_dev, list_pairs).reshape(N_DOM, N_REP, 2, H, W)
    to_lower = listed_rows[:, :, 0]
    to_upper = listed_rows[:, :, 1]
    empty_part = jnp.zeros((1, N_REP, H, W), jnp.bfloat16)
    from_lower = jnp.concatenate([empty_part, to_upper[:-1]], axis=0)
    from_upper = jnp.concatenate([to_lower[1:], empty_part], axis=0)
    halo_rows = jnp.concatenate([from_lower, from_upper], axis=2).reshape(N_DOM, N_REP * 2 * H, W)
    halo_ids = halo_block.reshape(N_DOM, N_REP * 2 * H)
    own_rows = elem_rows.reshape(N_DOM, N_REP * E_DEV, W)
    own_ids = elem_block.reshape(N_DOM, N_REP * E_DEV)
    row_pool = jnp.concatenate([own_rows, halo_rows], axis=1)
    pool_ids = jnp.concatenate([own_ids, halo_ids], axis=1)
    owner_codes = born_owner[:, 0]
    sorted_order = jnp.argsort(owner_codes, stable=True)
    window = NBLK * CAP
    sorted_rows = jnp.concatenate([born_rows[sorted_order], jnp.zeros((window, W), jnp.bfloat16)], axis=0)
    owner_counts = jax.ops.segment_sum(jnp.ones_like(owner_codes), owner_codes, NBLK).astype(jnp.int32)
    offsets = (jnp.cumsum(owner_counts) - owner_counts).astype(jnp.int32)
    mass_blocks = mass.reshape(NBLK, W)

    def factor_block(block_index):
        partition = block_index // N_REP
        block_id = block_index % N_REP
        row_data = row_pool[partition]
        in_block = pool_ids[partition] == block_id
        masked = jnp.where(in_block[:, None], row_data, jnp.zeros((), jnp.bfloat16))
        block_gram = jnp.dot(masked.T.astype(jnp.float32), row_data.astype(jnp.float32), preferred_element_type=jnp.float32)
        window_rows = lax.dynamic_slice_in_dim(sorted_rows, offsets[block_index].astype(jnp.int32), window, 0)
        live_rows = jnp.arange(window, dtype=jnp.int32) < owner_counts[block_index]
        born_masked = jnp.where(live_rows[:, None], window_rows, jnp.zeros((), jnp.bfloat16))
        block_gram = block_gram + jnp.dot(born_masked.T.astype(jnp.float32), window_rows.astype(jnp.float32), preferred_element_type=jnp.float32)
        system = jnp.diag(mass_blocks[block_index]) + block_gram / W
        return jnp.linalg.cholesky(system)
    factors = lax.map(factor_block, jnp.arange(NBLK, dtype=jnp.int32))
    return factors.reshape(NBLK * W, W)
```

```python
import functools

import jax
import jax.numpy as jnp
from jax import lax
from jax.experimental import pallas as pl
from jax.experimental.pallas import tpu as pltpu
from jax.sharding import PartitionSpec as P

CAP = 4
W = 512
TILE = 128
F32 = jnp.float32
BF16 = jnp.bfloat16
VMEM_LIMIT = 60 * 1024 * 1024
NT_DIMS = (((1,), (1,)), ((), ()))
HALF_A = ((0, 0, 0), (3, 384, 512))
HALF_B = ((1, 128, 0), (2, 256, 384))
HALF_W = 640


def call(kernel, outs, flops, *args, smem=(), scratch=(), name=None):
    specs = [
        pl.BlockSpec(memory_space=pltpu.SMEM if i in smem else pltpu.VMEM) for i in range(len(args))
    ]
    single = not isinstance(outs, (tuple, list))
    size = sum(a.size * a.dtype.itemsize for a in args)
    return pl.pallas_call(
        kernel,
        out_shape=outs,
        in_specs=specs,
        out_specs=pl.BlockSpec(memory_space=pltpu.VMEM)
        if single
        else [pl.BlockSpec(memory_space=pltpu.VMEM)] * len(outs),
        scratch_shapes=list(scratch),
        compiler_params=pltpu.CompilerParams(vmem_limit_bytes=VMEM_LIMIT),
        cost_estimate=pl.CostEstimate(flops=flops, bytes_accessed=size, transcendentals=0),
        name=name,
    )(*args)


def transposed(rows):
    order = lax.broadcasted_iota(jnp.int32, (W, W), 0) == lax.broadcasted_iota(jnp.int32, (W, W), 1)
    eye = jnp.where(order, 1.0, 0.0).astype(BF16)
    return lax.dot_general(eye, rows, NT_DIMS, preferred_element_type=F32).astype(BF16)


def pick_columns(cols_ref, list_ref, out_ref, first):
    total = cols_ref.shape[1]
    step = 256
    for c in range(0, out_ref.shape[1], step):
        names = list_ref[:, first + c : first + c + step]
        hot = lax.broadcasted_iota(jnp.int32, (total, step), 0) == names
        hot = jnp.where(hot, 1.0, 0.0).astype(BF16)
        out_ref[:, c : c + step] = jnp.dot(
            cols_ref[...], hot, preferred_element_type=F32
        ).astype(BF16)


def upper_list_kernel(rows_ref, list_ref, cols_ref, out_ref):
    for c in range(0, rows_ref.shape[0], 512):
        cols_ref[:, c : c + 512] = transposed(rows_ref[c : c + 512, :])
    pick_columns(cols_ref, list_ref, out_ref, out_ref.shape[1])


def lower_list_kernel(cols_ref, list_ref, out_ref):
    pick_columns(cols_ref, list_ref, out_ref, 0)


def pack_kernel(owner_ref, rows_ref, out_ref):
    owner = owner_ref[...]
    count = owner.shape[1]
    blocks = out_ref.shape[0] // CAP
    named = lax.broadcasted_iota(jnp.int32, (blocks, count), 0) == owner
    named = jnp.where(named, 1.0, 0.0)
    before = lax.broadcasted_iota(jnp.int32, (count, count), 0) < lax.broadcasted_iota(
        jnp.int32, (count, count), 1
    )
    before = jnp.where(before, 1.0, 0.0).astype(BF16)
    earlier = jnp.dot(named.astype(BF16), before, preferred_element_type=F32)
    rank = jnp.sum(named * earlier, axis=0, keepdims=True)
    place = owner * CAP + rank.astype(jnp.int32)
    hot = lax.broadcasted_iota(jnp.int32, (blocks * CAP, count), 0) == place
    hot = jnp.where(hot, 1.0, 0.0).astype(BF16)
    out_ref[...] = jnp.dot(hot, rows_ref[...], preferred_element_type=F32).astype(BF16)


def gram_into(out_ref, acc_ref, ids, half, pools):
    for panel, first, at in half:
        total = None
        width = W - first
        for cols_ref, block_ref in pools:
            left = cols_ref[panel * TILE : (panel + 1) * TILE, :]
            lefts = []
            for block in ids:
                keep = jnp.where(block_ref[...] == block, 1.0, 0.0).astype(BF16)
                lefts.append(left * keep)
            part = lax.dot_general(
                jnp.concatenate(lefts, axis=0),
                cols_ref[first:, :],
                NT_DIMS,
                preferred_element_type=F32,
            )
            total = part if total is None else total + part
        if acc_ref is not None:
            total = total + acc_ref[:, at : at + width]
        out_ref[:, at : at + width] = total


def elem_gram_kernel(rep_ref, cols_ref, block_ref, sa_ref, sb_ref, ka_ref, kb_ref):
    me = rep_ref[0]
    pair, mirror, far = me ^ 1, 3 - me, me ^ 2
    pools = [(cols_ref, block_ref)]
    gram_into(sa_ref, None, (pair, far), HALF_A, pools)
    gram_into(sb_ref, None, (mirror, far), HALF_B, pools)
    gram_into(ka_ref, None, (me, mirror), HALF_A, pools)
    gram_into(kb_ref, None, (me, pair), HALF_B, pools)


def halo_pools(lo_ref, up_ref, block_ref):
    half = lo_ref.shape[1]
    return [(lo_ref, block_ref.at[:, :half]), (up_ref, block_ref.at[:, half:])]


def sent_gram_kernel(rep_ref, lo_ref, up_ref, block_ref, a_ref, b_ref, sa_ref, sb_ref):
    me = rep_ref[0]
    pair, mirror, far = me ^ 1, 3 - me, me ^ 2
    pools = halo_pools(lo_ref, up_ref, block_ref)
    gram_into(sa_ref, a_ref, (pair, far), HALF_A, pools)
    gram_into(sb_ref, b_ref, (mirror, far), HALF_B, pools)


def kept_gram_kernel(rep_ref, lo_ref, up_ref, block_ref, a_ref, b_ref, ka_ref, kb_ref):
    me = rep_ref[0]
    pair, mirror = me ^ 1, 3 - me
    pools = halo_pools(lo_ref, up_ref, block_ref)
    gram_into(ka_ref, a_ref, (me, mirror), HALF_A, pools)
    gram_into(kb_ref, b_ref, (me, pair), HALF_B, pools)


def lane_copy(x, c):
    return jnp.broadcast_to(x[:, c : c + 1], (8, TILE))


def row_copy(x, i):
    return jnp.broadcast_to(x[i : i + 1, :], (8, TILE))


def add_all(xs):
    while len(xs) > 1:
        xs = [xs[i] + xs[i + 1] if i + 1 < len(xs) else xs[i] for i in range(0, len(xs), 2)]
    return xs[0]


def inverse_factor(columns):
    a = [[row_copy(columns[j], i) if i >= j else None for j in range(8)] for i in range(8)]
    low = [[None] * 8 for _ in range(8)]
    pivots = []
    for b in range(0, 8, 2):
        p, q, r = a[b][b], a[b + 1][b], a[b + 1][b + 1]
        det = p * r - q * q
        root, root_det = lax.rsqrt(p), lax.rsqrt(det)
        both = root * root_det
        pivots.append((root, -(q * both), p * both))
        for i in range(b + 2, 8):
            x, y = a[i][b], a[i][b + 1]
            low[i][b] = x * root
            low[i][b + 1] = (y * p - x * q) * both
        for i in range(b + 2, 8):
            for k in range(b + 2, i + 1):
                a[i][k] = a[i][k] - low[i][b] * low[k][b] - low[i][b + 1] * low[k][b + 1]
    inv = [[None] * 8 for _ in range(8)]
    for b in range(0, 8, 2):
        i0, i1, i2 = pivots[b // 2]
        inv[b][b], inv[b + 1][b], inv[b + 1][b + 1] = i0, i1, i2
        for m in range(b):
            s0 = add_all([low[b][k] * inv[k][m] for k in range(m, b)])
            s1 = add_all([low[b + 1][k] * inv[k][m] for k in range(m, b)])
            inv[b][m] = -(i0 * s0)
            inv[b + 1][m] = -(i1 * s0 + i2 * s1)
    return inv


def factor_panel(a_ref, tiles):
    sub = lax.broadcasted_iota(jnp.int32, (8, TILE), 0)
    lane = lax.broadcasted_iota(jnp.int32, (8, TILE), 1)
    cols = [slice(TILE * c, TILE * c + TILE) for c in range(tiles)]
    for s in range(16):
        o = 8 * s
        head = a_ref[o : o + 8, cols[0]]
        inv = inverse_factor([lane_copy(head, o + j) for j in range(8)])
        columns = []
        for m in range(8):
            v = inv[7][m]
            for i in range(6, m - 1, -1):
                v = jnp.where(sub <= i, inv[i][m], v)
            if m > 0:
                v = jnp.where(sub < m, 0.0, v)
            columns.append(v)
        upper = []
        for c in cols:
            x = a_ref[o : o + 8, c]
            upper.append(add_all([columns[m] * row_copy(x, m) for m in range(8)]))
        upper[0] = jnp.where(lane >= sub + o, upper[0], 0.0)
        for u, c in zip(upper, cols):
            a_ref[o : o + 8, c] = u
        if s == 15:
            break
        spread = [[row_copy(u, j) for j in range(8)] for u in upper]
        for g in range(s + 1, 16):
            rows = slice(8 * g, 8 * g + 8)
            x = a_ref[rows, cols[0]]
            b = [lane_copy(x, o + m) for m in range(8)]
            low = [add_all([inv[j][m] * b[m] for m in range(j + 1)]) for j in range(8)]
            for i, c in enumerate(cols):
                y = x if i == 0 else a_ref[rows, c]
                a_ref[rows, c] = y - add_all([low[j] * spread[i][j] for j in range(8)])


def factor_kernel(ka, ra, a2, kb, rb, b2, born, mass, out_ref, a_ref):
    pool = born[...]
    born_gram = lax.dot_general(pool, pool, (((0,), (0,)), ((), ())), preferred_element_type=F32)
    sub = lax.broadcasted_iota(jnp.int32, (TILE, TILE), 0)
    lane = lax.broadcasted_iota(jnp.int32, (TILE, TILE), 1)
    own = slice(0, TILE)
    for k0, r0, s0, half in ((ka, ra, a2, HALF_A), (kb, rb, b2, HALF_B)):
        for panel, first, at in half:
            cols = slice(at, at + W - first)
            rows = slice(panel * TILE, (panel + 1) * TILE)
            g = k0[own, cols] + r0[own, cols] + s0[:, cols] + born_gram[rows, first:]
            a_ref[rows, first:] = g * (1.0 / W)
    for k in range(4):
        rows = slice(TILE * k, TILE * (k + 1))
        first = TILE * k
        diag = a_ref[rows, rows]
        a_ref[rows, rows] = diag + jnp.where(sub == lane, mass[:, rows], 0.0)
        if k > 0:
            a_ref[rows, first:] = a_ref[rows, first:] - jnp.dot(
                out_ref[rows, :first],
                a_ref[:first, first:],
                precision=lax.Precision.HIGHEST,
                preferred_element_type=F32,
            )
            out_ref[: first, rows] = jnp.zeros((first, TILE), F32)
        factor_panel(a_ref.at[rows, first:], 4 - k)
        for c in range(k, 4):
            out_ref[TILE * c : TILE * (c + 1), rows] = a_ref[rows, TILE * c : TILE * (c + 1)].T


def local(elem_rows, elem_block, send_lists, halo_block, born_rows, born_owner, mass):
    rows = elem_rows.shape[0]
    listed = send_lists.shape[0] // 2
    dom_size, rep_size = lax.axis_size("dom"), lax.axis_size("rep")
    rep = lax.axis_index("rep").astype(jnp.int32).reshape(1)
    shape = jax.ShapeDtypeStruct
    lists = send_lists.reshape(1, -1)
    pick_flops = 2 * W * rows * listed

    cols, to_upper = call(
        upper_list_kernel,
        (shape((W, rows), BF16), shape((W, listed), BF16)),
        pick_flops + 2 * W * W * rows,
        elem_rows,
        lists,
        name="upper_list",
    )
    up = [(i, i + 1) for i in range(dom_size - 1)]
    down = [(j, i) for i, j in up]
    from_lower = lax.ppermute(to_upper, "dom", up)
    to_lower = call(
        lower_list_kernel, shape((W, listed), BF16), pick_flops, cols, lists, name="lower_list"
    )
    from_upper = lax.ppermute(to_lower, "dom", down)

    slots = dom_size * rep_size
    packed = call(
        pack_kernel,
        shape((slots * CAP, W), BF16),
        2 * slots * CAP * W * W,
        born_owner.reshape(1, -1),
        born_rows,
        name="pack_born",
    )
    arrived = lax.all_to_all(
        packed.reshape(slots, CAP, W), ("dom", "rep"), split_axis=0, concat_axis=0, tiled=True
    ).reshape(slots * CAP, W)

    part = shape((2 * TILE, HALF_W), F32)
    gram_flops = 4 * 6 * 2 * TILE * 256 * rows
    ids = elem_block.reshape(1, -1)
    sa, sb, ka, kb = call(
        elem_gram_kernel, (part,) * 4, gram_flops, rep, cols, ids, smem=(0,), name="elem_gram"
    )
    halo_ids = halo_block.reshape(1, -1)
    sa, sb = call(
        sent_gram_kernel,
        (part,) * 2,
        gram_flops // 2,
        rep,
        from_lower,
        from_upper,
        halo_ids,
        sa,
        sb,
        smem=(0,),
        name="sent_gram",
    )
    pair = [(i, i ^ 1) for i in range(rep_size)]
    mirror = [(i, 3 - i) for i in range(rep_size)]
    ra = lax.ppermute(sa, "rep", pair)
    rb = lax.ppermute(sb, "rep", mirror)
    ka, kb = call(
        kept_gram_kernel,
        (part,) * 2,
        gram_flops // 2,
        rep,
        from_lower,
        from_upper,
        halo_ids,
        ka,
        kb,
        smem=(0,),
        name="kept_gram",
    )
    a2 = lax.ppermute(ka[TILE:] + ra[TILE:], "rep", mirror)
    b2 = lax.ppermute(kb[TILE:] + rb[TILE:], "rep", pair)
    return call(
        factor_kernel,
        shape((W, W), F32),
        10**9,
        ka,
        ra,
        a2,
        kb,
        rb,
        b2,
        arrived,
        mass.reshape(1, -1),
        scratch=(pltpu.VMEM((W, W), F32),),
        name="factor",
    )


def solution(mesh):
    in_specs = (
        P(("dom", "rep"), None),
        P(("dom", "rep")),
        P(("dom", "rep")),
        P(("dom", "rep")),
        P(("dom", "rep"), None),
        P(("dom", "rep"), None),
        P(("dom", "rep")),
    )
    out_specs = P(("dom", "rep"), None)
    return jax.shard_map(local, mesh=mesh, in_specs=in_specs, out_specs=out_specs, check_vma=False)
```

```python
import functools

import jax
import jax.numpy as jnp
from jax import lax
from jax.experimental import pallas as pl
from jax.experimental.pallas import tpu as pltpu
from jax.sharding import PartitionSpec as P

CAP = 4
W = 512
TILE = 128
F32 = jnp.float32
BF16 = jnp.bfloat16
VMEM_LIMIT = 32 * 1024 * 1024
NT_DIMS = (((1,), (1,)), ((), ()))
HALF_A = ((0, 0, 0), (3, 384, 512))
HALF_B = ((1, 128, 0), (2, 256, 384))
HALF_W = 640


def call(kernel, outs, flops, *args, smem=(), anywhere=(), scratch=(), name=None):
    specs = [
        pl.BlockSpec(
            memory_space=pltpu.SMEM if i in smem else pl.ANY if i in anywhere else pltpu.VMEM
        )
        for i in range(len(args))
    ]
    single = not isinstance(outs, (tuple, list))
    size = sum(a.size * a.dtype.itemsize for a in args)
    return pl.pallas_call(
        kernel,
        out_shape=outs,
        in_specs=specs,
        out_specs=pl.BlockSpec(memory_space=pltpu.VMEM)
        if single
        else [pl.BlockSpec(memory_space=pltpu.VMEM)] * len(outs),
        scratch_shapes=list(scratch),
        compiler_params=pltpu.CompilerParams(vmem_limit_bytes=VMEM_LIMIT),
        cost_estimate=pl.CostEstimate(flops=flops, bytes_accessed=size, transcendentals=0),
        name=name,
    )(*args)


def transposed(rows):
    order = lax.broadcasted_iota(jnp.int32, (W, W), 0) == lax.broadcasted_iota(jnp.int32, (W, W), 1)
    eye = jnp.where(order, 1.0, 0.0).astype(BF16)
    return lax.dot_general(eye, rows, NT_DIMS, preferred_element_type=F32).astype(BF16)


def listed_kernel(rows_ref, list_ref, cols_ref, lower_ref, upper_ref):
    total, listed = rows_ref.shape[0], lower_ref.shape[1]
    for c in range(0, total, 512):
        cols_ref[:, c : c + 512] = transposed(rows_ref[c : c + 512, :])
    step, deep = 256, 256
    places = lax.broadcasted_iota(jnp.int32, (deep, step), 0).astype(BF16)
    for out_ref, first in ((upper_ref, listed), (lower_ref, 0)):
        for c in range(0, listed, step):
            names = list_ref[:, first + c : first + c + step]
            hot = []
            for h in range(0, total, deep):
                near = jnp.clip(names - h, -1, deep).astype(F32).astype(BF16)
                hot.append(jnp.where(places == near, 1.0, 0.0).astype(BF16))
            out_ref[:, c : c + step] = jnp.dot(
                cols_ref[...], jnp.concatenate(hot, axis=0), preferred_element_type=F32
            ).astype(BF16)


def pack_kernel(owner_ref, rows_ref, out_ref):
    owner = owner_ref[...]
    count = owner.shape[1]
    blocks = out_ref.shape[0]
    named = lax.broadcasted_iota(jnp.int32, (blocks, count), 0) == owner
    named = jnp.where(named, 1.0, 0.0)
    before = lax.broadcasted_iota(jnp.int32, (count, count), 0) < lax.broadcasted_iota(
        jnp.int32, (count, count), 1
    )
    before = jnp.where(before, 1.0, 0.0).astype(BF16)
    earlier = jnp.dot(named.astype(BF16), before, preferred_element_type=F32)
    rank = jnp.sum(named * earlier, axis=0, keepdims=True)
    place = owner * CAP + rank.astype(jnp.int32)
    hot = lax.broadcasted_iota(jnp.int32, (blocks * CAP, count), 0) == place
    hot = jnp.where(hot, 1.0, 0.0).astype(BF16)
    packed = jnp.dot(hot, rows_ref[...], preferred_element_type=F32).astype(BF16)
    out_ref[...] = packed.reshape(out_ref.shape)


def gram_kernel(kept, rep_ref, cols, lo, up, ids, halo_ids, a_ref, b_ref, buf, sems):
    me = rep_ref[0]
    pair, mirror, far = me ^ 1, 3 - me, me ^ 2
    for_a, for_b = ((me, mirror), (me, pair)) if kept else ((pair, far), (mirror, far))
    pieces, at = [], 0
    for i, ref in enumerate((cols, lo, up)):
        width = ref.shape[1]
        copy = pltpu.make_async_copy(ref, buf.at[:, at : at + width], sems.at[i])
        copy.start()
        pieces.append((copy, at, width))
        at += width
    own = cols.shape[1]
    right = left = None
    for copy, at, width in pieces:
        copy.wait()
        for c in range(at, at + width, 1024):
            ids_ref, k = (ids, c) if c < own else (halo_ids, c - own)
            names = ids_ref[:, k : k + 1024]
            masks_a = [jnp.where(names == b, 1.0, 0.0).astype(BF16) for b in for_a]
            masks_b = [jnp.where(names == b, 1.0, 0.0).astype(BF16) for b in for_b]
            part = []
            for panel, masks in ((0, masks_a), (1, masks_b), (3, masks_a), (2, masks_b)):
                x = buf[panel * TILE : (panel + 1) * TILE, c : c + 1024]
                part += [x * m for m in masks]
            part = jnp.concatenate(part, axis=0)
            r = lax.dot_general(
                part, buf[256:, c : c + 1024], NT_DIMS, preferred_element_type=F32
            )
            l = lax.dot_general(
                part[:512], buf[:256, c : c + 1024], NT_DIMS, preferred_element_type=F32
            )
            right = r if right is None else right + r
            left = l if left is None else left + l
    two = 2 * TILE
    a_ref[:, :256] = left[:two]
    a_ref[:, 256:512] = right[:two]
    a_ref[:, 512:] = right[2 * two : 3 * two, TILE:]
    b_ref[:, :TILE] = left[two:, TILE:]
    b_ref[:, TILE:384] = right[two : 2 * two]
    b_ref[:, 384:] = right[3 * two :]


def born_gram_kernel(pool_ref, out_ref):
    pool = pool_ref[...].reshape(-1, W)
    dims = (((0,), (0,)), ((), ()))
    out_ref[...] = lax.dot_general(pool, pool, dims, preferred_element_type=F32)


def lane_copy(x, c):
    return jnp.broadcast_to(x[:, c : c + 1], (8, TILE))


def row_copy(x, i):
    return jnp.broadcast_to(x[i : i + 1, :], (8, TILE))


def add_all(xs):
    while len(xs) > 1:
        xs = [xs[i] + xs[i + 1] if i + 1 < len(xs) else xs[i] for i in range(0, len(xs), 2)]
    return xs[0]


def inverse_factor(columns):
    a = [[row_copy(columns[j], i) if i >= j else None for j in range(8)] for i in range(8)]
    low = [[None] * 8 for _ in range(8)]
    pivots = []
    for b in range(0, 8, 2):
        p, q, r = a[b][b], a[b + 1][b], a[b + 1][b + 1]
        det = p * r - q * q
        root, root_det = lax.rsqrt(p), lax.rsqrt(det)
        both = root * root_det
        pivots.append((root, -(q * both), p * both))
        for i in range(b + 2, 8):
            x, y = a[i][b], a[i][b + 1]
            low[i][b] = x * root
            low[i][b + 1] = (y * p - x * q) * both
        for i in range(b + 2, 8):
            for k in range(b + 2, i + 1):
                a[i][k] = a[i][k] - low[i][b] * low[k][b] - low[i][b + 1] * low[k][b + 1]
    inv = [[None] * 8 for _ in range(8)]
    for b in range(0, 8, 2):
        i0, i1, i2 = pivots[b // 2]
        inv[b][b], inv[b + 1][b], inv[b + 1][b + 1] = i0, i1, i2
        for m in range(b):
            s0 = add_all([low[b][k] * inv[k][m] for k in range(m, b)])
            s1 = add_all([low[b + 1][k] * inv[k][m] for k in range(m, b)])
            inv[b][m] = -(i0 * s0)
            inv[b + 1][m] = -(i1 * s0 + i2 * s1)
    return inv


def factor_panel(a_ref, tiles):
    sub = lax.broadcasted_iota(jnp.int32, (8, TILE), 0)
    lane = lax.broadcasted_iota(jnp.int32, (8, TILE), 1)
    cols = [slice(TILE * c, TILE * c + TILE) for c in range(tiles)]
    for s in range(16):
        o = 8 * s
        head = a_ref[o : o + 8, cols[0]]
        inv = inverse_factor([lane_copy(head, o + j) for j in range(8)])
        columns = []
        for m in range(8):
            v = inv[7][m]
            for i in range(6, m - 1, -1):
                v = jnp.where(sub <= i, inv[i][m], v)
            if m > 0:
                v = jnp.where(sub < m, 0.0, v)
            columns.append(v)
        upper = []
        for c in cols:
            x = a_ref[o : o + 8, c]
            upper.append(add_all([columns[m] * row_copy(x, m) for m in range(8)]))
        upper[0] = jnp.where(lane >= sub + o, upper[0], 0.0)
        for u, c in zip(upper, cols):
            a_ref[o : o + 8, c] = u
        if s == 15:
            break
        spread = [[row_copy(u, j) for j in range(8)] for u in upper]
        for g in range(s + 1, 16):
            rows = slice(8 * g, 8 * g + 8)
            x = a_ref[rows, cols[0]]
            b = [lane_copy(x, o + m) for m in range(8)]
            low = [add_all([inv[j][m] * b[m] for m in range(j + 1)]) for j in range(8)]
            for i, c in enumerate(cols):
                y = x if i == 0 else a_ref[rows, c]
                a_ref[rows, c] = y - add_all([low[j] * spread[i][j] for j in range(8)])


def factor_kernel(ka, ra, a2, kb, rb, b2, born, mass, out_ref, a_ref):
    sub = lax.broadcasted_iota(jnp.int32, (TILE, TILE), 0)
    lane = lax.broadcasted_iota(jnp.int32, (TILE, TILE), 1)
    own = slice(0, TILE)
    for k0, r0, s0, half in ((ka, ra, a2, HALF_A), (kb, rb, b2, HALF_B)):
        for panel, first, at in half:
            cols = slice(at, at + W - first)
            rows = slice(panel * TILE, (panel + 1) * TILE)
            g = k0[own, cols] + r0[own, cols] + s0[:, cols] + born[rows, first:]
            a_ref[rows, first:] = g * (1.0 / W)
    for k in range(4):
        rows = slice(TILE * k, TILE * (k + 1))
        first = TILE * k
        diag = a_ref[rows, rows]
        a_ref[rows, rows] = diag + jnp.where(sub == lane, mass[:, rows], 0.0)
        if k > 0:
            a_ref[rows, first:] = a_ref[rows, first:] - jnp.dot(
                out_ref[rows, :first],
                a_ref[:first, first:],
                precision=lax.Precision.HIGHEST,
                preferred_element_type=F32,
            )
            out_ref[: first, rows] = jnp.zeros((first, TILE), F32)
        factor_panel(a_ref.at[rows, first:], 4 - k)
        for c in range(k, 4):
            out_ref[TILE * c : TILE * (c + 1), rows] = a_ref[rows, TILE * c : TILE * (c + 1)].T


def local(elem_rows, elem_block, send_lists, halo_block, born_rows, born_owner, mass):
    rows = elem_rows.shape[0]
    listed = send_lists.shape[0] // 2
    dom_size, rep_size = lax.axis_size("dom"), lax.axis_size("rep")
    rep = lax.axis_index("rep").astype(jnp.int32).reshape(1)
    shape = jax.ShapeDtypeStruct
    lists = send_lists.reshape(1, -1)
    narrow = shape((W, listed), BF16)
    cols, to_lower, to_upper = call(
        listed_kernel,
        (shape((W, rows), BF16), narrow, narrow),
        4 * W * rows * listed + 2 * W * W * rows,
        elem_rows,
        lists,
        name="listed",
    )
    up = [(i, i + 1) for i in range(dom_size - 1)]
    down = [(j, i) for i, j in up]
    from_lower = lax.ppermute(to_upper, "dom", up)
    from_upper = lax.ppermute(to_lower, "dom", down)

    slots = dom_size * rep_size
    packed = call(
        pack_kernel,
        shape((slots, CAP, W), BF16),
        2 * slots * CAP * W * W,
        born_owner.reshape(1, -1),
        born_rows,
        name="pack_born",
    )
    arrived = lax.all_to_all(packed, ("dom", "rep"), split_axis=0, concat_axis=0, tiled=True)
    born_gram = call(
        born_gram_kernel, shape((W, W), F32), 2 * slots * CAP * W * W, arrived, name="born_gram"
    )

    part = shape((2 * TILE, HALF_W), F32)

    def gram(kept):
        return call(
            functools.partial(gram_kernel, kept),
            (part,) * 2,
            2 * 6 * 2 * TILE * 256 * (rows + 2 * listed),
            rep,
            cols,
            from_lower,
            from_upper,
            elem_block.reshape(1, -1),
            halo_block.reshape(1, -1),
            smem=(0,),
            anywhere=(1, 2, 3),
            scratch=(
                pltpu.VMEM((W, rows + 2 * listed), BF16),
                pltpu.SemaphoreType.DMA((3,)),
            ),
            name="kept_gram" if kept else "sent_gram",
        )

    sa, sb = gram(False)
    pair = [(i, i ^ 1) for i in range(rep_size)]
    mirror = [(i, 3 - i) for i in range(rep_size)]
    ra = lax.ppermute(sa, "rep", pair)
    rb = lax.ppermute(sb, "rep", mirror)
    ka, kb = gram(True)
    a2 = lax.ppermute(ka[TILE:] + ra[TILE:], "rep", mirror)
    b2 = lax.ppermute(kb[TILE:] + rb[TILE:], "rep", pair)
    return call(
        factor_kernel,
        shape((W, W), F32),
        10**9,
        ka,
        ra,
        a2,
        kb,
        rb,
        b2,
        born_gram,
        mass.reshape(1, -1),
        scratch=(pltpu.VMEM((W, W), F32),),
        name="factor",
    )


def solution(mesh):
    in_specs = (
        P(("dom", "rep"), None),
        P(("dom", "rep")),
        P(("dom", "rep")),
        P(("dom", "rep")),
        P(("dom", "rep"), None),
        P(("dom", "rep"), None),
        P(("dom", "rep")),
    )
    out_specs = P(("dom", "rep"), None)
    return jax.shard_map(local, mesh=mesh, in_specs=in_specs, out_specs=out_specs, check_vma=False)
```

```python
import functools

import jax
import jax.numpy as jnp
from jax import lax
from jax.experimental import pallas as pl
from jax.experimental.pallas import tpu as pltpu
from jax.sharding import PartitionSpec as P

CAP = 4
W = 512
TILE = 128
F32 = jnp.float32
BF16 = jnp.bfloat16
VMEM_LIMIT = 32 * 1024 * 1024
VMEM_WHOLE = 63 * 1024 * 1024 + 512 * 1024
NT_DIMS = (((1,), (1,)), ((), ()))
HALF_A = ((0, 0, 0), (3, 384, 512))
HALF_B = ((1, 128, 0), (2, 256, 384))
HALF_W = 640


def call(kernel, outs, flops, *args, smem=(), anywhere=(), scratch=(), vmem=VMEM_WHOLE, name=None):
    specs = [
        pl.BlockSpec(
            memory_space=pltpu.SMEM if i in smem else pltpu.HBM if i in anywhere else pltpu.VMEM
        )
        for i in range(len(args))
    ]
    single = not isinstance(outs, (tuple, list))
    size = sum(a.size * a.dtype.itemsize for a in args)
    return pl.pallas_call(
        kernel,
        out_shape=outs,
        in_specs=specs,
        out_specs=pl.BlockSpec(memory_space=pltpu.VMEM)
        if single
        else [pl.BlockSpec(memory_space=pltpu.VMEM)] * len(outs),
        scratch_shapes=list(scratch),
        compiler_params=pltpu.CompilerParams(vmem_limit_bytes=vmem),
        cost_estimate=pl.CostEstimate(flops=flops, bytes_accessed=size, transcendentals=0),
        name=name,
    )(*args)


def transposed(rows):
    order = lax.broadcasted_iota(jnp.int32, (W, W), 0) == lax.broadcasted_iota(jnp.int32, (W, W), 1)
    eye = jnp.where(order, 1.0, 0.0).astype(BF16)
    return lax.dot_general(eye, rows, NT_DIMS, preferred_element_type=F32).astype(BF16)


def listed_kernel(rows_ref, list_ref, cols_ref, lower_ref, upper_ref, rows, sems):
    total, listed = rows_ref.shape[0], lower_ref.shape[1]
    piece = total // sems.shape[0]
    copies = []
    for i in range(sems.shape[0]):
        part = pl.ds(i * piece, piece)
        copies.append(pltpu.make_async_copy(rows_ref.at[part, :], rows.at[part, :], sems.at[i]))
        copies[-1].start()
    for i, copy in enumerate(copies):
        copy.wait()
        c = i * piece
        cols_ref[:, c : c + piece] = transposed(rows[c : c + piece, :])
    step, deep = 256, 256
    places = lax.broadcasted_iota(jnp.int32, (deep, step), 0).astype(BF16)
    for out_ref, first in ((upper_ref, listed), (lower_ref, 0)):
        for c in range(0, listed, step):
            names = list_ref[:, first + c : first + c + step]
            hot = []
            for h in range(0, total, deep):
                near = jnp.clip(names - h, -1, deep).astype(F32).astype(BF16)
                hot.append(jnp.where(places == near, 1.0, 0.0).astype(BF16))
            out_ref[:, c : c + step] = jnp.dot(
                cols_ref[...], jnp.concatenate(hot, axis=0), preferred_element_type=F32
            ).astype(BF16)


def pack_kernel(owner_ref, rows_ref, out_ref):
    owner = owner_ref[...]
    count = owner.shape[1]
    blocks = out_ref.shape[0]
    named = lax.broadcasted_iota(jnp.int32, (blocks, count), 0) == owner
    named = jnp.where(named, 1.0, 0.0)
    before = lax.broadcasted_iota(jnp.int32, (count, count), 0) < lax.broadcasted_iota(
        jnp.int32, (count, count), 1
    )
    before = jnp.where(before, 1.0, 0.0).astype(BF16)
    earlier = jnp.dot(named.astype(BF16), before, preferred_element_type=F32)
    rank = jnp.sum(named * earlier, axis=0, keepdims=True)
    place = owner * CAP + rank.astype(jnp.int32)
    hot = lax.broadcasted_iota(jnp.int32, (blocks * CAP, count), 0) == place
    hot = jnp.where(hot, 1.0, 0.0).astype(BF16)
    packed = jnp.dot(hot, rows_ref[...], preferred_element_type=F32).astype(BF16)
    out_ref[...] = packed.reshape(out_ref.shape)


def gram_kernel(kept, rep_ref, cols, lo, up, ids, halo_ids, a_ref, b_ref, buf, sems):
    me = rep_ref[0]
    pair, mirror, far = me ^ 1, 3 - me, me ^ 2
    for_a, for_b = ((me, mirror), (me, pair)) if kept else ((pair, far), (mirror, far))
    pieces, at = [], 0
    for i, ref in enumerate((cols, lo, up)):
        width = ref.shape[1]
        copy = pltpu.make_async_copy(ref, buf.at[:, at : at + width], sems.at[i])
        copy.start()
        pieces.append((copy, at, width))
        at += width
    own = cols.shape[1]
    right = left = None
    for copy, at, width in pieces:
        copy.wait()
        for c in range(at, at + width, 1024):
            ids_ref, k = (ids, c) if c < own else (halo_ids, c - own)
            names = ids_ref[:, k : k + 1024]
            masks_a = [jnp.where(names == b, 1.0, 0.0).astype(BF16) for b in for_a]
            masks_b = [jnp.where(names == b, 1.0, 0.0).astype(BF16) for b in for_b]
            part = []
            for panel, masks in ((0, masks_a), (1, masks_b), (3, masks_a), (2, masks_b)):
                x = buf[panel * TILE : (panel + 1) * TILE, c : c + 1024]
                part += [x * m for m in masks]
            part = jnp.concatenate(part, axis=0)
            r = lax.dot_general(
                part, buf[256:, c : c + 1024], NT_DIMS, preferred_element_type=F32
            )
            l = lax.dot_general(
                part[:512], buf[:256, c : c + 1024], NT_DIMS, preferred_element_type=F32
            )
            right = r if right is None else right + r
            left = l if left is None else left + l
    two = 2 * TILE
    a_ref[:, :256] = left[:two]
    a_ref[:, 256:512] = right[:two]
    a_ref[:, 512:] = right[2 * two : 3 * two, TILE:]
    b_ref[:, :TILE] = left[two:, TILE:]
    b_ref[:, TILE:384] = right[two : 2 * two]
    b_ref[:, 384:] = right[3 * two :]


def born_gram_kernel(pool_ref, out_ref):
    pool = pool_ref[...].reshape(-1, W)
    dims = (((0,), (0,)), ((), ()))
    out_ref[...] = lax.dot_general(pool, pool, dims, preferred_element_type=F32)


def lane_copy(x, c):
    return jnp.broadcast_to(x[:, c : c + 1], (8, TILE))


def row_copy(x, i):
    return jnp.broadcast_to(x[i : i + 1, :], (8, TILE))


def add_all(xs):
    while len(xs) > 1:
        xs = [xs[i] + xs[i + 1] if i + 1 < len(xs) else xs[i] for i in range(0, len(xs), 2)]
    return xs[0]


def inverse_factor(columns):
    a = [[row_copy(columns[j], i) if i >= j else None for j in range(8)] for i in range(8)]
    low = [[None] * 8 for _ in range(8)]
    pivots = []
    for b in range(0, 8, 2):
        p, q, r = a[b][b], a[b + 1][b], a[b + 1][b + 1]
        det = p * r - q * q
        root, root_det = lax.rsqrt(p), lax.rsqrt(det)
        both = root * root_det
        pivots.append((root, -(q * both), p * both))
        for i in range(b + 2, 8):
            x, y = a[i][b], a[i][b + 1]
            low[i][b] = x * root
            low[i][b + 1] = (y * p - x * q) * both
        for i in range(b + 2, 8):
            for k in range(b + 2, i + 1):
                a[i][k] = a[i][k] - low[i][b] * low[k][b] - low[i][b + 1] * low[k][b + 1]
    inv = [[None] * 8 for _ in range(8)]
    for b in range(0, 8, 2):
        i0, i1, i2 = pivots[b // 2]
        inv[b][b], inv[b + 1][b], inv[b + 1][b + 1] = i0, i1, i2
        for m in range(b):
            s0 = add_all([low[b][k] * inv[k][m] for k in range(m, b)])
            s1 = add_all([low[b + 1][k] * inv[k][m] for k in range(m, b)])
            inv[b][m] = -(i0 * s0)
            inv[b + 1][m] = -(i1 * s0 + i2 * s1)
    return inv


SUB = 64


def factor_panel(a_ref, tiles):
    sub = lax.broadcasted_iota(jnp.int32, (8, TILE), 0)
    lane = lax.broadcasted_iota(jnp.int32, (8, TILE), 1)
    cols = [slice(TILE * c, TILE * c + TILE) for c in range(tiles)]
    pivot = None
    for s in range(16):
        o = 8 * s
        last = (o // SUB + 1) * SUB // 8
        if pivot is None:
            head = a_ref[o : o + 8, cols[0]]
            pivot = [lane_copy(head, o + j) for j in range(8)]
        inv = inverse_factor(pivot)
        pivot = near = None
        if s + 1 < last:
            head = a_ref[o + 8 : o + 16, cols[0]]
            b = [lane_copy(head, o + m) for m in range(8)]
            own = [lane_copy(head, o + 8 + j) for j in range(8)]
            near = [add_all([inv[j][m] * b[m] for m in range(j + 1)]) for j in range(8)]
            pivot = [
                own[j] - add_all([near[m] * row_copy(near[m], j) for m in range(8)])
                for j in range(8)
            ]
        columns = []
        for m in range(8):
            v = inv[7][m]
            for i in range(6, m - 1, -1):
                v = jnp.where(sub <= i, inv[i][m], v)
            if m > 0:
                v = jnp.where(sub < m, 0.0, v)
            columns.append(v)
        upper = []
        for c in cols:
            x = a_ref[o : o + 8, c]
            upper.append(add_all([columns[m] * row_copy(x, m) for m in range(8)]))
        upper[0] = jnp.where(lane >= sub + o, upper[0], 0.0)
        for u, c in zip(upper, cols):
            a_ref[o : o + 8, c] = u
        if s + 1 < last:
            spread = [[row_copy(u, j) for j in range(8)] for u in upper]
            for g in range(s + 1, last):
                rows = slice(8 * g, 8 * g + 8)
                x = a_ref[rows, cols[0]]
                low = near
                if g > s + 1:
                    b = [lane_copy(x, o + m) for m in range(8)]
                    low = [add_all([inv[j][m] * b[m] for m in range(j + 1)]) for j in range(8)]
                for i, c in enumerate(cols):
                    y = x if i == 0 else a_ref[rows, c]
                    a_ref[rows, c] = y - add_all([low[j] * spread[i][j] for j in range(8)])
        elif s + 1 < 16:
            done = a_ref[o + 8 - SUB : o + 8, :]
            a_ref[o + 8 : TILE, :] = a_ref[o + 8 : TILE, :] - lax.dot_general(
                done[:, o + 8 : TILE],
                done,
                (((0,), (0,)), ((), ())),
                precision=lax.Precision.HIGHEST,
                preferred_element_type=F32,
            )


def factor_kernel(ka, ra, a2, kb, rb, b2, born, mass, out_ref, a_ref):
    sub = lax.broadcasted_iota(jnp.int32, (TILE, TILE), 0)
    lane = lax.broadcasted_iota(jnp.int32, (TILE, TILE), 1)
    own = slice(0, TILE)
    for k0, r0, s0, half in ((ka, ra, a2, HALF_A), (kb, rb, b2, HALF_B)):
        for panel, first, at in half:
            cols = slice(at, at + W - first)
            rows = slice(panel * TILE, (panel + 1) * TILE)
            g = k0[own, cols] + r0[own, cols] + s0[:, cols] + born[rows, first:]
            a_ref[rows, first:] = g * (1.0 / W)
    for k in range(4):
        rows = slice(TILE * k, TILE * (k + 1))
        first = TILE * k
        diag = a_ref[rows, rows]
        a_ref[rows, rows] = diag + jnp.where(sub == lane, mass[:, rows], 0.0)
        if k > 0:
            a_ref[rows, first:] = a_ref[rows, first:] - jnp.dot(
                out_ref[rows, :first],
                a_ref[:first, first:],
                precision=lax.Precision.HIGHEST,
                preferred_element_type=F32,
            )
            out_ref[: first, rows] = jnp.zeros((first, TILE), F32)
        factor_panel(a_ref.at[rows, first:], 4 - k)
        for c in range(k, 4):
            out_ref[TILE * c : TILE * (c + 1), rows] = a_ref[rows, TILE * c : TILE * (c + 1)].T


def local(elem_rows, elem_block, send_lists, halo_block, born_rows, born_owner, mass):
    rows = elem_rows.shape[0]
    listed = send_lists.shape[0] // 2
    dom_size, rep_size = lax.axis_size("dom"), lax.axis_size("rep")
    rep = lax.axis_index("rep").astype(jnp.int32).reshape(1)
    shape = jax.ShapeDtypeStruct
    lists = send_lists.reshape(1, -1)
    narrow = shape((W, listed), BF16)
    cols, to_lower, to_upper = call(
        listed_kernel,
        (shape((W, rows), BF16), narrow, narrow),
        4 * W * rows * listed + 2 * W * W * rows,
        elem_rows,
        lists,
        anywhere=(0,),
        scratch=(pltpu.VMEM((rows, W), BF16), pltpu.SemaphoreType.DMA((4,))),
        name="listed",
    )
    up = [(i, i + 1) for i in range(dom_size - 1)]
    down = [(j, i) for i, j in up]
    from_lower = lax.ppermute(to_upper, "dom", up)
    from_upper = lax.ppermute(to_lower, "dom", down)

    slots = dom_size * rep_size
    packed = call(
        pack_kernel,
        shape((slots, CAP, W), BF16),
        2 * slots * CAP * W * W,
        born_owner.reshape(1, -1),
        born_rows,
        name="pack_born",
    )
    arrived = lax.all_to_all(packed, ("dom", "rep"), split_axis=0, concat_axis=0, tiled=True)
    born_gram = call(
        born_gram_kernel, shape((W, W), F32), 2 * slots * CAP * W * W, arrived, vmem=VMEM_LIMIT, name="born_gram"
    )

    part = shape((2 * TILE, HALF_W), F32)

    def gram(kept):
        return call(
            functools.partial(gram_kernel, kept),
            (part,) * 2,
            2 * 6 * 2 * TILE * 256 * (rows + 2 * listed),
            rep,
            cols,
            from_lower,
            from_upper,
            elem_block.reshape(1, -1),
            halo_block.reshape(1, -1),
            smem=(0,),
            anywhere=(1, 2, 3),
            scratch=(
                pltpu.VMEM((W, rows + 2 * listed), BF16),
                pltpu.SemaphoreType.DMA((3,)),
            ),
            name="kept_gram" if kept else "sent_gram",
        )

    sa, sb = gram(False)
    pair = [(i, i ^ 1) for i in range(rep_size)]
    mirror = [(i, 3 - i) for i in range(rep_size)]
    ra = lax.ppermute(sa, "rep", pair)
    rb = lax.ppermute(sb, "rep", mirror)
    ka, kb = gram(True)
    a2 = lax.ppermute(ka[TILE:] + ra[TILE:], "rep", mirror)
    b2 = lax.ppermute(kb[TILE:] + rb[TILE:], "rep", pair)
    return call(
        factor_kernel,
        shape((W, W), F32),
        10**9,
        ka,
        ra,
        a2,
        kb,
        rb,
        b2,
        born_gram,
        mass.reshape(1, -1),
        scratch=(pltpu.VMEM((W, W), F32),),
        vmem=VMEM_LIMIT,
        name="factor",
    )


def solution(mesh):
    in_specs = (
        P(("dom", "rep"), None),
        P(("dom", "rep")),
        P(("dom", "rep")),
        P(("dom", "rep")),
        P(("dom", "rep"), None),
        P(("dom", "rep"), None),
        P(("dom", "rep")),
    )
    out_specs = P(("dom", "rep"), None)
    return jax.shard_map(local, mesh=mesh, in_specs=in_specs, out_specs=out_specs, check_vma=False)
```

```python
import functools

import jax
import jax.numpy as jnp
from jax import lax
from jax.experimental import pallas as pl
from jax.experimental.pallas import tpu as pltpu
from jax.sharding import PartitionSpec as P

CAP = 4
W = 512
TILE = 128
F32 = jnp.float32
BF16 = jnp.bfloat16
VMEM_LIMIT = 32 * 1024 * 1024
VMEM_WHOLE = 63 * 1024 * 1024 + 512 * 1024
NT_DIMS = (((1,), (1,)), ((), ()))
PLAIN = 2 * TILE
MIXED = 2 * TILE + 8


def call(kernel, outs, flops, *args, smem=(), anywhere=(), out_space=pltpu.VMEM, scratch=(), vmem=VMEM_WHOLE, name=None):
    specs = [
        pl.BlockSpec(
            memory_space=pltpu.SMEM if i in smem else pltpu.HBM if i in anywhere else pltpu.VMEM
        )
        for i in range(len(args))
    ]
    single = not isinstance(outs, (tuple, list))
    size = sum(a.size * a.dtype.itemsize for a in args)
    return pl.pallas_call(
        kernel,
        out_shape=outs,
        in_specs=specs,
        out_specs=pl.BlockSpec(memory_space=out_space)
        if single
        else [pl.BlockSpec(memory_space=out_space)] * len(outs),
        scratch_shapes=list(scratch),
        compiler_params=pltpu.CompilerParams(vmem_limit_bytes=vmem),
        cost_estimate=pl.CostEstimate(flops=flops, bytes_accessed=size, transcendentals=0),
        name=name,
    )(*args)


def transposed(rows):
    order = lax.broadcasted_iota(jnp.int32, (W, W), 0) == lax.broadcasted_iota(jnp.int32, (W, W), 1)
    eye = jnp.where(order, 1.0, 0.0).astype(BF16)
    return lax.dot_general(eye, rows, NT_DIMS, preferred_element_type=F32).astype(BF16)


def listed_kernel(
    rows_ref, list_ref, cols_out, lower_out, upper_out, rows, cols, lower, upper, in_sems, sems
):
    total, listed = rows.shape[0], lower.shape[1]
    piece = total // in_sems.shape[0]
    copies = []
    for i in range(in_sems.shape[0]):
        part = pl.ds(i * piece, piece)
        copies.append(pltpu.make_async_copy(rows_ref.at[part, :], rows.at[part, :], in_sems.at[i]))
        copies[-1].start()
    sent = []

    def send(source, target, c, width):
        part = pl.ds(c, width)
        sent.append(
            pltpu.make_async_copy(source.at[:, part], target.at[:, part], sems.at[len(sent)])
        )
        sent[-1].start()

    for i, copy in enumerate(copies):
        copy.wait()
        c = i * piece
        cols[:, c : c + piece] = transposed(rows[c : c + piece, :])
        send(cols, cols_out, c, piece)
    step, deep = 256, 256
    places = lax.broadcasted_iota(jnp.int32, (deep, step), 0).astype(BF16)
    for buf, target, first in ((upper, upper_out, listed), (lower, lower_out, 0)):
        for c in range(0, listed, step):
            names = list_ref[:, first + c : first + c + step]
            hot = []
            for h in range(0, total, deep):
                near = jnp.clip(names - h, -1, deep).astype(F32).astype(BF16)
                hot.append(jnp.where(places == near, 1.0, 0.0).astype(BF16))
            buf[:, c : c + step] = jnp.dot(
                cols[...], jnp.concatenate(hot, axis=0), preferred_element_type=F32
            ).astype(BF16)
            send(buf, target, c, step)
    for copy in sent:
        copy.wait()


def pack_kernel(owner_ref, rows_ref, out_ref):
    owner = owner_ref[...]
    count = owner.shape[1]
    blocks = out_ref.shape[0]
    named = lax.broadcasted_iota(jnp.int32, (blocks, count), 0) == owner
    named = jnp.where(named, 1.0, 0.0)
    before = lax.broadcasted_iota(jnp.int32, (count, count), 0) < lax.broadcasted_iota(
        jnp.int32, (count, count), 1
    )
    before = jnp.where(before, 1.0, 0.0).astype(BF16)
    earlier = jnp.dot(named.astype(BF16), before, preferred_element_type=F32)
    rank = jnp.sum(named * earlier, axis=0, keepdims=True)
    place = owner * CAP + rank.astype(jnp.int32)
    hot = lax.broadcasted_iota(jnp.int32, (blocks * CAP, count), 0) == place
    hot = jnp.where(hot, 1.0, 0.0).astype(BF16)
    packed = jnp.dot(hot, rows_ref[...], preferred_element_type=F32).astype(BF16)
    out_ref[...] = packed.reshape(out_ref.shape)


LEFT = {1: ((0, "a"), (1, "a")), 2: ()}
RIGHT = {1: ((0, "b"),), 2: ((1, "a"), (2, "b"), (3, "b"))}


def place_pair(out_ref, at, first, second, between):
    sub = lax.broadcasted_iota(jnp.int32, (TILE, TILE), 0)
    lane = lax.broadcasted_iota(jnp.int32, (TILE, TILE), 1)
    out_ref[at : at + TILE, :] = jnp.where(lane >= sub, first, second)
    out_ref[at + TILE : at + 2 * TILE, :] = between
    diagonal = jnp.sum(jnp.where(lane == sub, second, 0.0), axis=0, keepdims=True)
    out_ref[at + 2 * TILE : at + MIXED, :] = jnp.broadcast_to(diagonal, (8, TILE))


def gram_kernel(kept, parts, rep_ref, cols, lo, up, ids, halo_ids, after, *refs):
    outs, (buf, sems) = refs[: 2 * len(parts)], refs[2 * len(parts) :]
    me = rep_ref[0]
    pair, mirror, far = me ^ 1, 3 - me, me ^ 2
    blocks = {
        "a": (me, mirror) if kept else (pair, far),
        "b": (me, pair) if kept else (mirror, far),
    }
    half, own = lo.shape[1], cols.shape[1]
    pieces = []
    for ref, begin, widths in (
        (cols, 0, (512, 512, 1024)),
        (lo, own, (half,)),
        (up, own + half, (half,)),
    ):
        at = 0
        for width in widths:
            copy = pltpu.make_async_copy(
                ref.at[:, pl.ds(at, width)],
                buf.at[:, pl.ds(begin + at, width)],
                sems.at[len(pieces)],
            )
            copy.start()
            pieces.append((copy, begin + at, width))
            at += width
    left_rows = [r for part in parts for r in LEFT[part]]
    right_rows = [r for part in parts for r in RIGHT[part]]
    left = right = None
    for copy, c, width in pieces:
        copy.wait()
        span = slice(c, c + width)
        names = ids[:, span] if c < own else halo_ids[:, c - own : c - own + width]
        masks = {
            k: [jnp.where(names == block, 1.0, 0.0).astype(BF16) for block in v]
            for k, v in blocks.items()
        }
        part = {}
        for panel, k in dict.fromkeys(left_rows + right_rows):
            x = buf[panel * TILE : (panel + 1) * TILE, span]
            part[panel, k] = [x * m for m in masks[k]]

        def product(rows, columns):
            stack = jnp.concatenate([x for r in rows for x in part[r]], axis=0)
            return lax.dot_general(
                stack, buf[columns, span], NT_DIMS, preferred_element_type=F32
            )

        r = product(right_rows, slice(256, 512))
        right = r if right is None else right + r
        if left_rows:
            l = product(left_rows, slice(0, 256))
            left = l if left is None else left + l

    def tiles(value, rows, which, i):
        at = (2 * rows.index(which) + i) * TILE
        return value[at : at + TILE, :TILE], value[at : at + TILE, TILE:]

    for part, a_ref, b_ref in zip(parts, outs[::2], outs[1::2]):
        for i in range(2):
            if part == 1:
                first, between = tiles(left, left_rows, (0, "a"), i)
                _, second = tiles(left, left_rows, (1, "a"), i)
                place_pair(a_ref, i * MIXED, first, second, between)
                plain_ref, plain = b_ref, tiles(right, right_rows, (0, "b"), i)
            else:
                first, between = tiles(right, right_rows, (2, "b"), i)
                _, second = tiles(right, right_rows, (3, "b"), i)
                place_pair(b_ref, i * MIXED, first, second, between)
                plain_ref, plain = a_ref, tiles(right, right_rows, (1, "a"), i)
            for j in range(2):
                at = i * PLAIN + j * TILE
                plain_ref[at : at + TILE, :] = plain[j]


def born_gram_kernel(pool_ref, out_ref):
    pool = pool_ref[...].reshape(-1, W)
    dims = (((0,), (0,)), ((), ()))
    out_ref[...] = lax.dot_general(pool, pool, dims, preferred_element_type=F32)


def lane_copy(x, c):
    return jnp.broadcast_to(x[:, c : c + 1], (8, TILE))


def row_copy(x, i):
    return jnp.broadcast_to(x[i : i + 1, :], (8, TILE))


def add_all(xs):
    while len(xs) > 1:
        xs = [xs[i] + xs[i + 1] if i + 1 < len(xs) else xs[i] for i in range(0, len(xs), 2)]
    return xs[0]


def inverse_factor(columns):
    a = [[row_copy(columns[j], i) if i >= j else None for j in range(8)] for i in range(8)]
    low = [[None] * 8 for _ in range(8)]
    pivots = []
    for b in range(0, 8, 2):
        p, q, r = a[b][b], a[b + 1][b], a[b + 1][b + 1]
        det = p * r - q * q
        root, root_det = lax.rsqrt(p), lax.rsqrt(det)
        both = root * root_det
        pivots.append((root, -(q * both), p * both))
        for i in range(b + 2, 8):
            x, y = a[i][b], a[i][b + 1]
            low[i][b] = x * root
            low[i][b + 1] = (y * p - x * q) * both
        for i in range(b + 2, 8):
            for k in range(b + 2, i + 1):
                a[i][k] = a[i][k] - low[i][b] * low[k][b] - low[i][b + 1] * low[k][b + 1]
    inv = [[None] * 8 for _ in range(8)]
    for b in range(0, 8, 2):
        i0, i1, i2 = pivots[b // 2]
        inv[b][b], inv[b + 1][b], inv[b + 1][b + 1] = i0, i1, i2
        for m in range(b):
            s0 = add_all([low[b][k] * inv[k][m] for k in range(m, b)])
            s1 = add_all([low[b + 1][k] * inv[k][m] for k in range(m, b)])
            inv[b][m] = -(i0 * s0)
            inv[b + 1][m] = -(i1 * s0 + i2 * s1)
    return inv


SUB = 64


def factor_panel(a_ref, tiles):
    sub = lax.broadcasted_iota(jnp.int32, (8, TILE), 0)
    lane = lax.broadcasted_iota(jnp.int32, (8, TILE), 1)
    cols = [slice(TILE * c, TILE * c + TILE) for c in range(tiles)]
    pivot = None
    for s in range(16):
        o = 8 * s
        last = (o // SUB + 1) * SUB // 8
        if pivot is None:
            head = a_ref[o : o + 8, cols[0]]
            pivot = [lane_copy(head, o + j) for j in range(8)]
        inv = inverse_factor(pivot)
        pivot = near = None
        if s + 1 < last:
            head = a_ref[o + 8 : o + 16, cols[0]]
            b = [lane_copy(head, o + m) for m in range(8)]
            own = [lane_copy(head, o + 8 + j) for j in range(8)]
            near = [add_all([inv[j][m] * b[m] for m in range(j + 1)]) for j in range(8)]
            pivot = [
                own[j] - add_all([near[m] * row_copy(near[m], j) for m in range(8)])
                for j in range(8)
            ]
        columns = []
        for m in range(8):
            v = inv[7][m]
            for i in range(6, m - 1, -1):
                v = jnp.where(sub <= i, inv[i][m], v)
            if m > 0:
                v = jnp.where(sub < m, 0.0, v)
            columns.append(v)
        upper = []
        for c in cols:
            x = a_ref[o : o + 8, c]
            upper.append(add_all([columns[m] * row_copy(x, m) for m in range(8)]))
        upper[0] = jnp.where(lane >= sub + o, upper[0], 0.0)
        for u, c in zip(upper, cols):
            a_ref[o : o + 8, c] = u
        if s + 1 < last:
            spread = [[row_copy(u, j) for j in range(8)] for u in upper]
            for g in range(s + 1, last):
                rows = slice(8 * g, 8 * g + 8)
                x = a_ref[rows, cols[0]]
                low = near
                if g > s + 1:
                    b = [lane_copy(x, o + m) for m in range(8)]
                    low = [add_all([inv[j][m] * b[m] for m in range(j + 1)]) for j in range(8)]
                for i, c in enumerate(cols):
                    y = x if i == 0 else a_ref[rows, c]
                    a_ref[rows, c] = y - add_all([low[j] * spread[i][j] for j in range(8)])
        elif s + 1 < 16:
            done = a_ref[o + 8 - SUB : o + 8, :]
            a_ref[o + 8 : TILE, :] = a_ref[o + 8 : TILE, :] - lax.dot_general(
                done[:, o + 8 : TILE],
                done,
                (((0,), (0,)), ((), ())),
                precision=lax.Precision.HIGHEST,
                preferred_element_type=F32,
            )


def onward_kernel(ka, ra, kb, rb, after, a_ref, b_ref):
    a_size, b_size = a_ref.shape[0], b_ref.shape[0]
    a_ref[...] = ka[a_size:, :] + ra[a_size:, :]
    b_ref[...] = kb[b_size:, :] + rb[b_size:, :]


def tile_sum(kept, come, last, at):
    span = slice(at, at + TILE)
    return kept[span, :] + come[span, :] + last[span, :]


def split_pair(kept, come, last):
    sub = lax.broadcasted_iota(jnp.int32, (TILE, TILE), 0)
    lane = lax.broadcasted_iota(jnp.int32, (TILE, TILE), 1)
    both = tile_sum(kept, come, last, 0)
    flip = both.T
    row = slice(2 * TILE, 2 * TILE + 1)
    diagonal = kept[row, :] + come[row, :] + last[row, :]
    second = jnp.where(lane < sub, both, jnp.where(lane == sub, diagonal, flip))
    return jnp.where(lane >= sub, both, flip), second


def system_tile(gram, born, mass, k, c):
    rows, cols = slice(TILE * k, TILE * (k + 1)), slice(TILE * c, TILE * (c + 1))
    value = (gram + born[rows, cols]) * (1.0 / W)
    if k == c:
        sub = lax.broadcasted_iota(jnp.int32, (TILE, TILE), 0)
        lane = lax.broadcasted_iota(jnp.int32, (TILE, TILE), 1)
        value = value + jnp.where(sub == lane, mass[:, rows], 0.0)
    return value


def first_panel_kernel(ka, ra, a2, kb, rb, b2, born, mass, top_ref, next_ref):
    first, second = split_pair(ka, ra, a2)
    top = [first, tile_sum(ka, ra, a2, TILE), tile_sum(kb, rb, b2, 0), tile_sum(kb, rb, b2, TILE)]
    for c in range(4):
        top_ref[:, TILE * c : TILE * (c + 1)] = system_tile(top[c], born, mass, 0, c)
    next_ref[...] = system_tile(second, born, mass, 1, 1)
    factor_panel(top_ref, 4)


def other_panels_kernel(ka, ra, a2, kb, rb, b2, born, mass, top_ref, next_ref, out_ref, a_ref):
    third, fourth = split_pair(kb, rb, b2)
    grams = {
        (1, 2): tile_sum(ka, ra, a2, 0),
        (1, 3): tile_sum(ka, ra, a2, TILE),
        (2, 2): third,
        (2, 3): tile_sum(kb, rb, b2, TILE),
        (3, 3): fourth,
    }
    a_ref[:TILE, :] = top_ref[...]
    a_ref[TILE : 2 * TILE, TILE : 2 * TILE] = next_ref[...]
    for (k, c), gram in grams.items():
        a_ref[TILE * k : TILE * (k + 1), TILE * c : TILE * (c + 1)] = system_tile(
            gram, born, mass, k, c
        )
    for k in range(4):
        rows = slice(TILE * k, TILE * (k + 1))
        first = TILE * k
        if k > 0:
            a_ref[rows, first:] = a_ref[rows, first:] - jnp.dot(
                out_ref[rows, :first],
                a_ref[:first, first:],
                precision=lax.Precision.HIGHEST,
                preferred_element_type=F32,
            )
            out_ref[:first, rows] = jnp.zeros((first, TILE), F32)
            factor_panel(a_ref.at[rows, first:], 4 - k)
        for c in range(k, 4):
            out_ref[TILE * c : TILE * (c + 1), rows] = a_ref[rows, TILE * c : TILE * (c + 1)].T


def local(elem_rows, elem_block, send_lists, halo_block, born_rows, born_owner, mass):
    rows = elem_rows.shape[0]
    listed = send_lists.shape[0] // 2
    dom_size, rep_size = lax.axis_size("dom"), lax.axis_size("rep")
    rep = lax.axis_index("rep").astype(jnp.int32).reshape(1)
    shape = jax.ShapeDtypeStruct
    lists = send_lists.reshape(1, -1)
    narrow = shape((W, listed), BF16)
    cols, to_lower, to_upper = call(
        listed_kernel,
        (shape((W, rows), BF16), narrow, narrow),
        4 * W * rows * listed + 2 * W * W * rows,
        elem_rows,
        lists,
        anywhere=(0,),
        out_space=pltpu.HBM,
        scratch=(
            pltpu.VMEM((rows, W), BF16),
            pltpu.VMEM((W, rows), BF16),
            pltpu.VMEM((W, listed), BF16),
            pltpu.VMEM((W, listed), BF16),
            pltpu.SemaphoreType.DMA((4,)),
            pltpu.SemaphoreType.DMA((12,)),
        ),
        name="listed",
    )
    up = [(i, i + 1) for i in range(dom_size - 1)]
    down = [(j, i) for i, j in up]
    from_lower = lax.ppermute(to_upper, "dom", up)
    from_upper = lax.ppermute(to_lower, "dom", down)

    slots = dom_size * rep_size
    packed = call(
        pack_kernel,
        shape((slots, CAP, W), BF16),
        2 * slots * CAP * W * W,
        born_owner.reshape(1, -1),
        born_rows,
        name="pack_born",
    )
    arrived = lax.all_to_all(packed, ("dom", "rep"), split_axis=0, concat_axis=0, tiled=True)
    born_gram = call(
        born_gram_kernel, shape((W, W), F32), 2 * slots * CAP * W * W, arrived, vmem=VMEM_LIMIT, name="born_gram"
    )

    mixed, plain = shape((2 * MIXED, TILE), F32), shape((2 * PLAIN, TILE), F32)
    halves = {1: (mixed, plain), 2: (plain, mixed)}

    def gram(kept, parts, after, name):
        return call(
            functools.partial(gram_kernel, kept, parts),
            tuple(half for part in parts for half in halves[part]),
            3 * 6 * 2 * TILE * 256 * (rows + 2 * listed) * len(parts),
            rep,
            cols,
            from_lower,
            from_upper,
            elem_block.reshape(1, -1),
            halo_block.reshape(1, -1),
            after,
            smem=(0,),
            anywhere=(1, 2, 3, 6),
            scratch=(
                pltpu.VMEM((W, rows + 2 * listed), BF16),
                pltpu.SemaphoreType.DMA((5,)),
            ),
            name=name,
        )

    pair = [(i, i ^ 1) for i in range(rep_size)]
    mirror = [(i, 3 - i) for i in range(rep_size)]
    come, after = {}, packed
    for part, name in ((1, "sent_gram_1"), (2, "sent_gram_2")):
        a, b = gram(False, (part,), after, name)
        after = a
        come[part] = lax.ppermute(a, "rep", pair), lax.ppermute(b, "rep", mirror)
    ka1, kb1, ka2, kb2 = gram(True, (1, 2), after, "kept_gram")
    pieces = {}
    after = ka2
    for part, ka, kb in ((1, ka1, kb1), (2, ka2, kb2)):
        ra, rb = come[part]
        a_size, b_size = ka.shape[0] // 2, kb.shape[0] // 2
        a_next, b_next = call(
            onward_kernel,
            (shape((a_size, TILE), F32), shape((b_size, TILE), F32)),
            10**6,
            ka,
            ra,
            kb,
            rb,
            after,
            anywhere=(4,),
            name=f"onward_{part}",
        )
        after = a_next
        a2 = lax.ppermute(a_next, "rep", mirror)
        b2 = lax.ppermute(b_next, "rep", pair)
        pieces[part] = ka, ra, a2, kb, rb, b2
    mass_row = mass.reshape(1, -1)
    top, following = call(
        first_panel_kernel,
        (shape((TILE, W), F32), shape((TILE, TILE), F32)),
        10**9,
        *pieces[1],
        born_gram,
        mass_row,
        vmem=VMEM_LIMIT,
        name="first_panel",
    )
    return call(
        other_panels_kernel,
        shape((W, W), F32),
        2 * 10**9,
        *pieces[2],
        born_gram,
        mass_row,
        top,
        following,
        scratch=(pltpu.VMEM((W, W), F32),),
        vmem=VMEM_LIMIT,
        name="other_panels",
    )


def solution(mesh):
    in_specs = (
        P(("dom", "rep"), None),
        P(("dom", "rep")),
        P(("dom", "rep")),
        P(("dom", "rep")),
        P(("dom", "rep"), None),
        P(("dom", "rep"), None),
        P(("dom", "rep")),
    )
    out_specs = P(("dom", "rep"), None)
    return jax.shard_map(local, mesh=mesh, in_specs=in_specs, out_specs=out_specs, check_vma=False)
```

```python
import functools

import jax
import jax.numpy as jnp
from jax import lax
from jax.experimental import pallas as pl
from jax.experimental.pallas import tpu as pltpu
from jax.sharding import PartitionSpec as P

CAP = 4
W = 512
TILE = 128
F32 = jnp.float32
BF16 = jnp.bfloat16
VMEM_LIMIT = 24 * 1024 * 1024
VMEM_WHOLE = 63 * 1024 * 1024 + 512 * 1024
NT_DIMS = (((1,), (1,)), ((), ()))
PLAIN = 2 * TILE
MIXED = 2 * TILE + 8


def call(kernel, outs, flops, *args, smem=(), anywhere=(), out_space=pltpu.VMEM, scratch=(), vmem=VMEM_LIMIT, name=None):
    specs = [
        pl.BlockSpec(
            memory_space=pltpu.SMEM if i in smem else pltpu.HBM if i in anywhere else pltpu.VMEM
        )
        for i in range(len(args))
    ]
    single = not isinstance(outs, (tuple, list))
    size = sum(a.size * a.dtype.itemsize for a in args)
    return pl.pallas_call(
        kernel,
        out_shape=outs,
        in_specs=specs,
        out_specs=pl.BlockSpec(memory_space=out_space)
        if single
        else [pl.BlockSpec(memory_space=out_space)] * len(outs),
        scratch_shapes=list(scratch),
        compiler_params=pltpu.CompilerParams(vmem_limit_bytes=vmem),
        cost_estimate=pl.CostEstimate(flops=flops, bytes_accessed=size, transcendentals=0),
        name=name,
    )(*args)


def listed_kernel(
    rows_ref, list_ref, cols_out, lower_out, upper_out, rows, cols, lower, upper, in_sems, sems
):
    total, listed = rows.shape[0], lower.shape[1]
    piece = total // in_sems.shape[0]
    copies = []
    for i in range(in_sems.shape[0]):
        part = pl.ds(i * piece, piece)
        copies.append(pltpu.make_async_copy(rows_ref.at[part, :], rows.at[part, :], in_sems.at[i]))
        copies[-1].start()
    sent = []

    def send(source, target, c, width):
        part = pl.ds(c, width)
        sent.append(
            pltpu.make_async_copy(source.at[:, part], target.at[:, part], sems.at[len(sent)])
        )
        sent[-1].start()

    for i, copy in enumerate(copies):
        copy.wait()
        c = i * piece
        cols[:, c : c + piece] = rows[c : c + piece, :].T
        send(cols, cols_out, c, piece)
    step, deep = 256, 256
    places = lax.broadcasted_iota(jnp.int32, (deep, step), 0).astype(BF16)
    for buf, target, first in ((upper, upper_out, listed), (lower, lower_out, 0)):
        for c in range(0, listed, step):
            names = list_ref[:, first + c : first + c + step]
            hot = []
            for h in range(0, total, deep):
                near = jnp.clip(names - h, -1, deep).astype(F32).astype(BF16)
                hot.append(jnp.maximum(1 - jnp.abs(places - near), 0).astype(BF16))
            buf[:, c : c + step] = jnp.dot(
                cols[...], jnp.concatenate(hot, axis=0), preferred_element_type=F32
            ).astype(BF16)
            send(buf, target, c, step)
    for copy in sent:
        copy.wait()


def pack_kernel(owner_ref, rows_ref, out_ref):
    owner = owner_ref[...]
    count = owner.shape[1]
    blocks = out_ref.shape[0]
    named = lax.broadcasted_iota(jnp.int32, (blocks, count), 0) == owner
    named = jnp.where(named, 1.0, 0.0)
    before = lax.broadcasted_iota(jnp.int32, (count, count), 0) < lax.broadcasted_iota(
        jnp.int32, (count, count), 1
    )
    before = jnp.where(before, 1.0, 0.0).astype(BF16)
    earlier = jnp.dot(named.astype(BF16), before, preferred_element_type=F32)
    rank = jnp.sum(named * earlier, axis=0, keepdims=True)
    place = owner * CAP + rank.astype(jnp.int32)
    hot = lax.broadcasted_iota(jnp.int32, (blocks * CAP, count), 0) == place
    hot = jnp.where(hot, 1.0, 0.0).astype(BF16)
    packed = jnp.dot(hot, rows_ref[...], preferred_element_type=F32).astype(BF16)
    out_ref[...] = packed.reshape(out_ref.shape)


LEFT = {1: ((0, "a"), (1, "a")), 2: ()}
RIGHT = {1: ((0, "b"),), 2: ((1, "a"), (2, "b"), (3, "b"))}


def place_pair(out_ref, at, first, second, between):
    sub = lax.broadcasted_iota(jnp.int32, (TILE, TILE), 0)
    lane = lax.broadcasted_iota(jnp.int32, (TILE, TILE), 1)
    out_ref[at : at + TILE, :] = jnp.where(lane >= sub, first, second)
    out_ref[at + TILE : at + 2 * TILE, :] = between
    diagonal = jnp.sum(jnp.where(lane == sub, second, 0.0), axis=0, keepdims=True)
    out_ref[at + 2 * TILE : at + MIXED, :] = jnp.broadcast_to(diagonal, (8, TILE))


def gram_kernel(kept, parts, rep_ref, cols, lo, up, ids, halo_ids, after, *outs):
    me = rep_ref[0]
    pair, mirror, far = me ^ 1, 3 - me, me ^ 2
    blocks = {
        "a": (me, mirror) if kept else (pair, far),
        "b": (me, pair) if kept else (mirror, far),
    }
    half, own = lo.shape[1], cols.shape[1]
    pieces = [(cols, ids, c) for c in range(0, own, 1024)]
    pieces += [(lo, halo_ids.at[:, :half], 0), (up, halo_ids.at[:, half:], 0)]
    left_rows = [r for part in parts for r in LEFT[part]]
    right_rows = [r for part in parts for r in RIGHT[part]]
    left = right = None
    for buf, names_ref, c in pieces:
        span = slice(c, c + 1024)
        names = names_ref[:, span]
        masks = {
            k: [jnp.where(names == block, 1.0, 0.0).astype(BF16) for block in v]
            for k, v in blocks.items()
        }
        part = {}
        for panel, k in dict.fromkeys(left_rows + right_rows):
            x = buf[panel * TILE : (panel + 1) * TILE, span]
            part[panel, k] = [x * m for m in masks[k]]

        def product(rows, columns):
            stack = jnp.concatenate([x for r in rows for x in part[r]], axis=0)
            return lax.dot_general(
                stack, buf[columns, span], NT_DIMS, preferred_element_type=F32
            )

        r = product(right_rows, slice(256, 512))
        right = r if right is None else right + r
        if left_rows:
            l = product(left_rows, slice(0, 256))
            left = l if left is None else left + l

    def tiles(value, rows, which, i):
        at = (2 * rows.index(which) + i) * TILE
        return value[at : at + TILE, :TILE], value[at : at + TILE, TILE:]

    for part, a_ref, b_ref in zip(parts, outs[::2], outs[1::2]):
        for i in range(2):
            if part == 1:
                first, between = tiles(left, left_rows, (0, "a"), i)
                _, second = tiles(left, left_rows, (1, "a"), i)
                place_pair(a_ref, i * MIXED, first, second, between)
                plain_ref, plain = b_ref, tiles(right, right_rows, (0, "b"), i)
            else:
                first, between = tiles(right, right_rows, (2, "b"), i)
                _, second = tiles(right, right_rows, (3, "b"), i)
                place_pair(b_ref, i * MIXED, first, second, between)
                plain_ref, plain = a_ref, tiles(right, right_rows, (1, "a"), i)
            for j in range(2):
                at = i * PLAIN + j * TILE
                plain_ref[at : at + TILE, :] = plain[j]


def born_gram_kernel(pool_ref, out_ref):
    pool = pool_ref[...].reshape(-1, W)
    dims = (((0,), (0,)), ((), ()))
    out_ref[...] = lax.dot_general(pool, pool, dims, preferred_element_type=F32)


def lane_copy(x, c):
    return jnp.broadcast_to(x[:, c : c + 1], (8, TILE))


def row_copy(x, i):
    return jnp.broadcast_to(x[i : i + 1, :], (8, TILE))


def add_all(xs):
    while len(xs) > 1:
        xs = [xs[i] + xs[i + 1] if i + 1 < len(xs) else xs[i] for i in range(0, len(xs), 2)]
    return xs[0]


def inverse_factor(columns):
    a = [[row_copy(columns[j], i) if i >= j else None for j in range(8)] for i in range(8)]
    low = [[None] * 8 for _ in range(8)]
    pivots = []
    for b in range(0, 8, 2):
        p, q, r = a[b][b], a[b + 1][b], a[b + 1][b + 1]
        det = p * r - q * q
        root, root_det = lax.rsqrt(p), lax.rsqrt(det)
        both = root * root_det
        pivots.append((root, -(q * both), p * both))
        for i in range(b + 2, 8):
            x, y = a[i][b], a[i][b + 1]
            low[i][b] = x * root
            low[i][b + 1] = (y * p - x * q) * both
        for i in range(b + 2, 8):
            for k in range(b + 2, i + 1):
                a[i][k] = a[i][k] - low[i][b] * low[k][b] - low[i][b + 1] * low[k][b + 1]
    inv = [[None] * 8 for _ in range(8)]
    for b in range(0, 8, 2):
        i0, i1, i2 = pivots[b // 2]
        inv[b][b], inv[b + 1][b], inv[b + 1][b + 1] = i0, i1, i2
        for m in range(b):
            s0 = add_all([low[b][k] * inv[k][m] for k in range(m, b)])
            s1 = add_all([low[b + 1][k] * inv[k][m] for k in range(m, b)])
            inv[b][m] = -(i0 * s0)
            inv[b + 1][m] = -(i1 * s0 + i2 * s1)
    return inv


SUB = 64


def factor_panel(a_ref, tiles):
    sub = lax.broadcasted_iota(jnp.int32, (8, TILE), 0)
    lane = lax.broadcasted_iota(jnp.int32, (8, TILE), 1)
    cols = [slice(TILE * c, TILE * c + TILE) for c in range(tiles)]
    pivot = None
    for s in range(16):
        o = 8 * s
        last = (o // SUB + 1) * SUB // 8
        if pivot is None:
            head = a_ref[o : o + 8, cols[0]]
            pivot = [lane_copy(head, o + j) for j in range(8)]
        inv = inverse_factor(pivot)
        pivot = near = None
        if s + 1 < last:
            head = a_ref[o + 8 : o + 16, cols[0]]
            b = [lane_copy(head, o + m) for m in range(8)]
            own = [lane_copy(head, o + 8 + j) for j in range(8)]
            near = [add_all([inv[j][m] * b[m] for m in range(j + 1)]) for j in range(8)]
            pivot = [
                own[j] - add_all([near[m] * row_copy(near[m], j) for m in range(8)])
                for j in range(8)
            ]
        columns = []
        for m in range(8):
            v = inv[7][m]
            for i in range(6, m - 1, -1):
                v = jnp.where(sub <= i, inv[i][m], v)
            if m > 0:
                v = jnp.where(sub < m, 0.0, v)
            columns.append(v)
        upper = []
        for c in cols:
            x = a_ref[o : o + 8, c]
            upper.append(add_all([columns[m] * row_copy(x, m) for m in range(8)]))
        upper[0] = jnp.where(lane >= sub + o, upper[0], 0.0)
        for u, c in zip(upper, cols):
            a_ref[o : o + 8, c] = u
        if s + 1 < last:
            spread = [[row_copy(u, j) for j in range(8)] for u in upper]
            for g in range(s + 1, last):
                rows = slice(8 * g, 8 * g + 8)
                x = a_ref[rows, cols[0]]
                low = near
                if g > s + 1:
                    b = [lane_copy(x, o + m) for m in range(8)]
                    low = [add_all([inv[j][m] * b[m] for m in range(j + 1)]) for j in range(8)]
                for i, c in enumerate(cols):
                    y = x if i == 0 else a_ref[rows, c]
                    a_ref[rows, c] = y - add_all([low[j] * spread[i][j] for j in range(8)])
        elif s + 1 < 16:
            done = a_ref[o + 8 - SUB : o + 8, :]
            a_ref[o + 8 : TILE, :] = a_ref[o + 8 : TILE, :] - lax.dot_general(
                done[:, o + 8 : TILE],
                done,
                (((0,), (0,)), ((), ())),
                precision=lax.Precision.HIGHEST,
                preferred_element_type=F32,
            )


def onward_kernel(ka, ra, kb, rb, after, a_ref, b_ref):
    a_size, b_size = a_ref.shape[0], b_ref.shape[0]
    a_ref[...] = ka[a_size:, :] + ra[a_size:, :]
    b_ref[...] = kb[b_size:, :] + rb[b_size:, :]


def tile_sum(kept, come, last, at):
    span = slice(at, at + TILE)
    return kept[span, :] + come[span, :] + last[span, :]


def split_pair(kept, come, last):
    sub = lax.broadcasted_iota(jnp.int32, (TILE, TILE), 0)
    lane = lax.broadcasted_iota(jnp.int32, (TILE, TILE), 1)
    both = tile_sum(kept, come, last, 0)
    flip = both.T
    row = slice(2 * TILE, 2 * TILE + 1)
    diagonal = kept[row, :] + come[row, :] + last[row, :]
    second = jnp.where(lane < sub, both, jnp.where(lane == sub, diagonal, flip))
    return jnp.where(lane >= sub, both, flip), second


def system_tile(gram, born, mass, k, c):
    rows, cols = slice(TILE * k, TILE * (k + 1)), slice(TILE * c, TILE * (c + 1))
    value = (gram + born[rows, cols]) * (1.0 / W)
    if k == c:
        sub = lax.broadcasted_iota(jnp.int32, (TILE, TILE), 0)
        lane = lax.broadcasted_iota(jnp.int32, (TILE, TILE), 1)
        value = value + jnp.where(sub == lane, mass[:, rows], 0.0)
    return value


def first_panel_kernel(ka, ra, a2, kb, rb, b2, born, mass, top_ref, next_ref):
    first, second = split_pair(ka, ra, a2)
    top = [first, tile_sum(ka, ra, a2, TILE), tile_sum(kb, rb, b2, 0), tile_sum(kb, rb, b2, TILE)]
    for c in range(4):
        top_ref[:, TILE * c : TILE * (c + 1)] = system_tile(top[c], born, mass, 0, c)
    next_ref[...] = system_tile(second, born, mass, 1, 1)
    factor_panel(top_ref, 4)


def other_panels_kernel(ka, ra, a2, kb, rb, b2, born, mass, top_ref, next_ref, out_ref, a_ref):
    third, fourth = split_pair(kb, rb, b2)
    grams = {
        (1, 2): tile_sum(ka, ra, a2, 0),
        (1, 3): tile_sum(ka, ra, a2, TILE),
        (2, 2): third,
        (2, 3): tile_sum(kb, rb, b2, TILE),
        (3, 3): fourth,
    }
    a_ref[:TILE, :] = top_ref[...]
    a_ref[TILE : 2 * TILE, TILE : 2 * TILE] = next_ref[...]
    for (k, c), gram in grams.items():
        a_ref[TILE * k : TILE * (k + 1), TILE * c : TILE * (c + 1)] = system_tile(
            gram, born, mass, k, c
        )
    for k in range(4):
        rows = slice(TILE * k, TILE * (k + 1))
        first = TILE * k
        if k > 0:
            a_ref[rows, first:] = a_ref[rows, first:] - jnp.dot(
                out_ref[rows, :first],
                a_ref[:first, first:],
                precision=lax.Precision.HIGHEST,
                preferred_element_type=F32,
            )
            out_ref[:first, rows] = jnp.zeros((first, TILE), F32)
            factor_panel(a_ref.at[rows, first:], 4 - k)
        for c in range(k, 4):
            out_ref[TILE * c : TILE * (c + 1), rows] = a_ref[rows, TILE * c : TILE * (c + 1)].T


def local(elem_rows, elem_block, send_lists, halo_block, born_rows, born_owner, mass):
    rows = elem_rows.shape[0]
    listed = send_lists.shape[0] // 2
    dom_size, rep_size = lax.axis_size("dom"), lax.axis_size("rep")
    rep = lax.axis_index("rep").astype(jnp.int32).reshape(1)
    shape = jax.ShapeDtypeStruct
    lists = send_lists.reshape(1, -1)
    narrow = shape((W, listed), BF16)
    cols, to_lower, to_upper = call(
        listed_kernel,
        (shape((W, rows), BF16), narrow, narrow),
        4 * W * rows * listed + 2 * W * W * rows,
        elem_rows,
        lists,
        anywhere=(0,),
        out_space=pltpu.HBM,
        vmem=VMEM_WHOLE,
        scratch=(
            pltpu.VMEM((rows, W), BF16),
            pltpu.VMEM((W, rows), BF16),
            pltpu.VMEM((W, listed), BF16),
            pltpu.VMEM((W, listed), BF16),
            pltpu.SemaphoreType.DMA((4,)),
            pltpu.SemaphoreType.DMA((12,)),
        ),
        name="listed",
    )
    up = [(i, i + 1) for i in range(dom_size - 1)]
    down = [(j, i) for i, j in up]
    from_lower = lax.ppermute(to_upper, "dom", up)
    from_upper = lax.ppermute(to_lower, "dom", down)

    slots = dom_size * rep_size
    packed = call(
        pack_kernel,
        shape((slots, CAP, W), BF16),
        2 * slots * CAP * W * W,
        born_owner.reshape(1, -1),
        born_rows,
        name="pack_born",
    )
    arrived = lax.all_to_all(packed, ("dom", "rep"), split_axis=0, concat_axis=0, tiled=True)
    born_gram = call(
        born_gram_kernel, shape((W, W), F32), 2 * slots * CAP * W * W, arrived, name="born_gram"
    )

    mixed, plain = shape((2 * MIXED, TILE), F32), shape((2 * PLAIN, TILE), F32)
    halves = {1: (mixed, plain), 2: (plain, mixed)}

    def gram(kept, parts, after, name):
        return call(
            functools.partial(gram_kernel, kept, parts),
            tuple(half for part in parts for half in halves[part]),
            3 * 6 * 2 * TILE * 256 * (rows + 2 * listed) * len(parts),
            rep,
            cols,
            from_lower,
            from_upper,
            elem_block.reshape(1, -1),
            halo_block.reshape(1, -1),
            after,
            smem=(0,),
            anywhere=(6,),
            name=name,
        )

    pair = [(i, i ^ 1) for i in range(rep_size)]
    mirror = [(i, 3 - i) for i in range(rep_size)]
    come, after = {}, packed
    for part, name in ((1, "sent_gram_1"), (2, "sent_gram_2")):
        a, b = gram(False, (part,), after, name)
        after = a
        come[part] = lax.ppermute(a, "rep", pair), lax.ppermute(b, "rep", mirror)
    ka1, kb1, ka2, kb2 = gram(True, (1, 2), after, "kept_gram")
    pieces = {}
    after = ka2
    for part, ka, kb in ((1, ka1, kb1), (2, ka2, kb2)):
        ra, rb = come[part]
        a_size, b_size = ka.shape[0] // 2, kb.shape[0] // 2
        a_next, b_next = call(
            onward_kernel,
            (shape((a_size, TILE), F32), shape((b_size, TILE), F32)),
            10**6,
            ka,
            ra,
            kb,
            rb,
            after,
            anywhere=(4,),
            name=f"onward_{part}",
        )
        after = a_next
        a2 = lax.ppermute(a_next, "rep", mirror)
        b2 = lax.ppermute(b_next, "rep", pair)
        pieces[part] = ka, ra, a2, kb, rb, b2
    mass_row = mass.reshape(1, -1)
    top, following = call(
        first_panel_kernel,
        (shape((TILE, W), F32), shape((TILE, TILE), F32)),
        10**9,
        *pieces[1],
        born_gram,
        mass_row,
        name="first_panel",
    )
    return call(
        other_panels_kernel,
        shape((W, W), F32),
        2 * 10**9,
        *pieces[2],
        born_gram,
        mass_row,
        top,
        following,
        scratch=(pltpu.VMEM((W, W), F32),),
        name="other_panels",
    )


def solution(mesh):
    in_specs = (
        P(("dom", "rep"), None),
        P(("dom", "rep")),
        P(("dom", "rep")),
        P(("dom", "rep")),
        P(("dom", "rep"), None),
        P(("dom", "rep"), None),
        P(("dom", "rep")),
    )
    out_specs = P(("dom", "rep"), None)
    return jax.shard_map(local, mesh=mesh, in_specs=in_specs, out_specs=out_specs, check_vma=False)
```

```python
import functools

import jax
import jax.numpy as jnp
from jax import lax
from jax.experimental import pallas as pl
from jax.experimental.pallas import tpu as pltpu
from jax.sharding import PartitionSpec as P

CAP = 4
W = 512
TILE = 128
F32 = jnp.float32
BF16 = jnp.bfloat16
VMEM_LIMIT = 24 * 1024 * 1024
VMEM_MOST = 64 * 1024 * 1024 - 2304 * 1024
VMEM_WHOLE = 63 * 1024 * 1024 + 512 * 1024
NT_DIMS = (((1,), (1,)), ((), ()))
PLAIN = 2 * TILE
MIXED = 2 * TILE + 8


def call(kernel, outs, flops, *args, smem=(), anywhere=(), out_space=pltpu.VMEM, scratch=(), vmem=VMEM_LIMIT, name=None):
    specs = [
        pl.BlockSpec(
            memory_space=pltpu.SMEM if i in smem else pltpu.HBM if i in anywhere else pltpu.VMEM
        )
        for i in range(len(args))
    ]
    single = not isinstance(outs, (tuple, list))
    size = sum(a.size * a.dtype.itemsize for a in args)
    return pl.pallas_call(
        kernel,
        out_shape=outs,
        in_specs=specs,
        out_specs=pl.BlockSpec(memory_space=out_space)
        if single
        else [pl.BlockSpec(memory_space=out_space)] * len(outs),
        scratch_shapes=list(scratch),
        compiler_params=pltpu.CompilerParams(vmem_limit_bytes=vmem),
        cost_estimate=pl.CostEstimate(flops=flops, bytes_accessed=size, transcendentals=0),
        name=name,
    )(*args)


def listed_kernel(
    rows_ref, list_ref, cols_out, lower_out, upper_out, rows, cols, lower, upper, in_sems, sems
):
    total, listed = rows.shape[0], lower.shape[1]
    piece = total // in_sems.shape[0]
    copies = []
    for i in range(in_sems.shape[0]):
        part = pl.ds(i * piece, piece)
        copies.append(pltpu.make_async_copy(rows_ref.at[part, :], rows.at[part, :], in_sems.at[i]))
        copies[-1].start()
    sent = []

    def send(source, target, c, width):
        part = pl.ds(c, width)
        sent.append(
            pltpu.make_async_copy(source.at[:, part], target.at[:, part], sems.at[len(sent)])
        )
        sent[-1].start()

    for i, copy in enumerate(copies):
        copy.wait()
        c = i * piece
        cols[:, c : c + piece] = rows[c : c + piece, :].T
        send(cols, cols_out, c, piece)
    step, deep = 256, 256
    places = lax.broadcasted_iota(jnp.int32, (deep, step), 0).astype(BF16)
    for buf, target, first in ((upper, upper_out, listed), (lower, lower_out, 0)):
        for c in range(0, listed, step):
            names = list_ref[:, first + c : first + c + step]
            hot = []
            for h in range(0, total, deep):
                near = jnp.clip(names - h, -1, deep).astype(F32).astype(BF16)
                hot.append(jnp.maximum(1 - jnp.abs(places - near), 0).astype(BF16))
            buf[:, c : c + step] = jnp.dot(
                cols[...], jnp.concatenate(hot, axis=0), preferred_element_type=F32
            ).astype(BF16)
            send(buf, target, c, step)
    for copy in sent:
        copy.wait()


def pack_kernel(owner_ref, rows_ref, out_ref, rows, sem):
    copy = pltpu.make_async_copy(rows_ref, rows, sem)
    copy.start()
    owner = owner_ref[...]
    count = owner.shape[1]
    blocks = out_ref.shape[0]
    named = lax.broadcasted_iota(jnp.int32, (blocks, count), 0) == owner
    named = jnp.where(named, 1.0, 0.0)
    before = lax.broadcasted_iota(jnp.int32, (count, count), 0) < lax.broadcasted_iota(
        jnp.int32, (count, count), 1
    )
    before = jnp.where(before, 1.0, 0.0).astype(BF16)
    earlier = jnp.dot(named.astype(BF16), before, preferred_element_type=F32)
    rank = jnp.sum(named * earlier, axis=0, keepdims=True)
    place = owner * CAP + rank.astype(jnp.int32)
    hot = lax.broadcasted_iota(jnp.int32, (blocks * CAP, count), 0) == place
    hot = jnp.where(hot, 1.0, 0.0).astype(BF16)
    copy.wait()
    packed = jnp.dot(hot, rows[...], preferred_element_type=F32).astype(BF16)
    out_ref[...] = packed.reshape(out_ref.shape)


LEFT = {1: ((0, "a"), (1, "a")), 2: ()}
RIGHT = {1: ((0, "b"),), 2: ((1, "a"), (2, "b"), (3, "b"))}


def place_pair(out_ref, at, first, second, between):
    sub = lax.broadcasted_iota(jnp.int32, (TILE, TILE), 0)
    lane = lax.broadcasted_iota(jnp.int32, (TILE, TILE), 1)
    out_ref[at : at + TILE, :] = jnp.where(lane >= sub, first, second)
    out_ref[at + TILE : at + 2 * TILE, :] = between
    diagonal = jnp.sum(jnp.where(lane == sub, second, 0.0), axis=0, keepdims=True)
    out_ref[at + 2 * TILE : at + MIXED, :] = jnp.broadcast_to(diagonal, (8, TILE))


def gram_kernel(kept, parts, rep_ref, cols, lo, up, ids, halo_ids, after, *outs):
    me = rep_ref[0]
    pair, mirror, far = me ^ 1, 3 - me, me ^ 2
    blocks = {
        "a": (me, mirror) if kept else (pair, far),
        "b": (me, pair) if kept else (mirror, far),
    }
    half, own = lo.shape[1], cols.shape[1]
    pieces = [(cols, ids, c) for c in range(0, own, 1024)]
    pieces += [(lo, halo_ids.at[:, :half], 0), (up, halo_ids.at[:, half:], 0)]
    left_rows = [r for part in parts for r in LEFT[part]]
    right_rows = [r for part in parts for r in RIGHT[part]]
    left = right = None
    for buf, names_ref, c in pieces:
        span = slice(c, c + 1024)
        names = names_ref[:, span]
        masks = {
            k: [jnp.where(names == block, 1.0, 0.0).astype(BF16) for block in v]
            for k, v in blocks.items()
        }
        part = {}
        for panel, k in dict.fromkeys(left_rows + right_rows):
            x = buf[panel * TILE : (panel + 1) * TILE, span]
            part[panel, k] = [x * m for m in masks[k]]

        def product(rows, columns):
            stack = jnp.concatenate([x for r in rows for x in part[r]], axis=0)
            return lax.dot_general(
                stack, buf[columns, span], NT_DIMS, preferred_element_type=F32
            )

        r = product(right_rows, slice(256, 512))
        right = r if right is None else right + r
        if left_rows:
            l = product(left_rows, slice(0, 256))
            left = l if left is None else left + l

    def tiles(value, rows, which, i):
        at = (2 * rows.index(which) + i) * TILE
        return value[at : at + TILE, :TILE], value[at : at + TILE, TILE:]

    for part, a_ref, b_ref in zip(parts, outs[::2], outs[1::2]):
        for i in range(2):
            if part == 1:
                first, between = tiles(left, left_rows, (0, "a"), i)
                _, second = tiles(left, left_rows, (1, "a"), i)
                place_pair(a_ref, i * MIXED, first, second, between)
                plain_ref, plain = b_ref, tiles(right, right_rows, (0, "b"), i)
            else:
                first, between = tiles(right, right_rows, (2, "b"), i)
                _, second = tiles(right, right_rows, (3, "b"), i)
                place_pair(b_ref, i * MIXED, first, second, between)
                plain_ref, plain = a_ref, tiles(right, right_rows, (1, "a"), i)
            for j in range(2):
                at = i * PLAIN + j * TILE
                plain_ref[at : at + TILE, :] = plain[j]


def born_gram_kernel(pool_ref, out_ref):
    pool = pool_ref[...].reshape(-1, W)
    dims = (((0,), (0,)), ((), ()))
    out_ref[...] = lax.dot_general(pool, pool, dims, preferred_element_type=F32)


def lane_copy(x, c):
    return jnp.broadcast_to(x[:, c : c + 1], (8, TILE))


def row_copy(x, i):
    return jnp.broadcast_to(x[i : i + 1, :], (8, TILE))


def add_all(xs):
    while len(xs) > 1:
        xs = [xs[i] + xs[i + 1] if i + 1 < len(xs) else xs[i] for i in range(0, len(xs), 2)]
    return xs[0]


def inverse_factor(columns):
    a = [[row_copy(columns[j], i) if i >= j else None for j in range(8)] for i in range(8)]
    low = [[None] * 8 for _ in range(8)]
    pivots = []
    for b in range(0, 8, 2):
        p, q, r = a[b][b], a[b + 1][b], a[b + 1][b + 1]
        det = p * r - q * q
        root, root_det = lax.rsqrt(p), lax.rsqrt(det)
        both = root * root_det
        pivots.append((root, -(q * both), p * both))
        for i in range(b + 2, 8):
            x, y = a[i][b], a[i][b + 1]
            low[i][b] = x * root
            low[i][b + 1] = (y * p - x * q) * both
        for i in range(b + 2, 8):
            for k in range(b + 2, i + 1):
                a[i][k] = a[i][k] - low[i][b] * low[k][b] - low[i][b + 1] * low[k][b + 1]
    inv = [[None] * 8 for _ in range(8)]
    for b in range(0, 8, 2):
        i0, i1, i2 = pivots[b // 2]
        inv[b][b], inv[b + 1][b], inv[b + 1][b + 1] = i0, i1, i2
        for m in range(b):
            s0 = add_all([low[b][k] * inv[k][m] for k in range(m, b)])
            s1 = add_all([low[b + 1][k] * inv[k][m] for k in range(m, b)])
            inv[b][m] = -(i0 * s0)
            inv[b + 1][m] = -(i1 * s0 + i2 * s1)
    return inv


SUB = 64


def factor_panel(a_ref, tiles):
    sub = lax.broadcasted_iota(jnp.int32, (8, TILE), 0)
    lane = lax.broadcasted_iota(jnp.int32, (8, TILE), 1)
    cols = [slice(TILE * c, TILE * c + TILE) for c in range(tiles)]
    pivot = None
    for s in range(16):
        o = 8 * s
        last = (o // SUB + 1) * SUB // 8
        if pivot is None:
            head = a_ref[o : o + 8, cols[0]]
            pivot = [lane_copy(head, o + j) for j in range(8)]
        inv = inverse_factor(pivot)
        pivot = near = None
        if s + 1 < last:
            head = a_ref[o + 8 : o + 16, cols[0]]
            b = [lane_copy(head, o + m) for m in range(8)]
            own = [lane_copy(head, o + 8 + j) for j in range(8)]
            near = [add_all([inv[j][m] * b[m] for m in range(j + 1)]) for j in range(8)]
            pivot = [
                own[j] - add_all([near[m] * row_copy(near[m], j) for m in range(8)])
                for j in range(8)
            ]
        columns = []
        for m in range(8):
            v = inv[7][m]
            for i in range(6, m - 1, -1):
                v = jnp.where(sub <= i, inv[i][m], v)
            if m > 0:
                v = jnp.where(sub < m, 0.0, v)
            columns.append(v)
        upper = []
        for c in cols:
            x = a_ref[o : o + 8, c]
            upper.append(add_all([columns[m] * row_copy(x, m) for m in range(8)]))
        upper[0] = jnp.where(lane >= sub + o, upper[0], 0.0)
        for u, c in zip(upper, cols):
            a_ref[o : o + 8, c] = u
        if s + 1 < last:
            spread = [[row_copy(u, j) for j in range(8)] for u in upper]
            for g in range(s + 1, last):
                rows = slice(8 * g, 8 * g + 8)
                x = a_ref[rows, cols[0]]
                low = near
                if g > s + 1:
                    b = [lane_copy(x, o + m) for m in range(8)]
                    low = [add_all([inv[j][m] * b[m] for m in range(j + 1)]) for j in range(8)]
                for i, c in enumerate(cols):
                    y = x if i == 0 else a_ref[rows, c]
                    a_ref[rows, c] = y - add_all([low[j] * spread[i][j] for j in range(8)])
        elif s + 1 < 16:
            done = a_ref[o + 8 - SUB : o + 8, :]
            a_ref[o + 8 : TILE, :] = a_ref[o + 8 : TILE, :] - lax.dot_general(
                done[:, o + 8 : TILE],
                done,
                (((0,), (0,)), ((), ())),
                precision=lax.Precision.HIGHEST,
                preferred_element_type=F32,
            )


def onward_kernel(ka, ra, kb, rb, after, a_ref, b_ref):
    a_size, b_size = a_ref.shape[0], b_ref.shape[0]
    a_ref[...] = ka[a_size:, :] + ra[a_size:, :]
    b_ref[...] = kb[b_size:, :] + rb[b_size:, :]


def tile_sum(kept, come, last, at):
    span = slice(at, at + TILE)
    return kept[span, :] + come[span, :] + last[span, :]


def split_pair(kept, come, last):
    sub = lax.broadcasted_iota(jnp.int32, (TILE, TILE), 0)
    lane = lax.broadcasted_iota(jnp.int32, (TILE, TILE), 1)
    both = tile_sum(kept, come, last, 0)
    flip = both.T
    row = slice(2 * TILE, 2 * TILE + 1)
    diagonal = kept[row, :] + come[row, :] + last[row, :]
    second = jnp.where(lane < sub, both, jnp.where(lane == sub, diagonal, flip))
    return jnp.where(lane >= sub, both, flip), second


def system_tile(gram, born, mass, k, c):
    rows, cols = slice(TILE * k, TILE * (k + 1)), slice(TILE * c, TILE * (c + 1))
    value = (gram + born[rows, cols]) * (1.0 / W)
    if k == c:
        sub = lax.broadcasted_iota(jnp.int32, (TILE, TILE), 0)
        lane = lax.broadcasted_iota(jnp.int32, (TILE, TILE), 1)
        value = value + jnp.where(sub == lane, mass[:, rows], 0.0)
    return value


def first_panel_kernel(ka, ra, a2, kb, rb, b2, born, mass, top_ref, next_ref):
    first, second = split_pair(ka, ra, a2)
    top = [first, tile_sum(ka, ra, a2, TILE), tile_sum(kb, rb, b2, 0), tile_sum(kb, rb, b2, TILE)]
    for c in range(4):
        top_ref[:, TILE * c : TILE * (c + 1)] = system_tile(top[c], born, mass, 0, c)
    next_ref[...] = system_tile(second, born, mass, 1, 1)
    factor_panel(top_ref, 4)


def other_panels_kernel(ka, ra, a2, kb, rb, b2, born, mass, top_ref, next_ref, out_ref, a_ref):
    third, fourth = split_pair(kb, rb, b2)
    grams = {
        (1, 2): tile_sum(ka, ra, a2, 0),
        (1, 3): tile_sum(ka, ra, a2, TILE),
        (2, 2): third,
        (2, 3): tile_sum(kb, rb, b2, TILE),
        (3, 3): fourth,
    }
    a_ref[:TILE, :] = top_ref[...]
    a_ref[TILE : 2 * TILE, TILE : 2 * TILE] = next_ref[...]
    for (k, c), gram in grams.items():
        a_ref[TILE * k : TILE * (k + 1), TILE * c : TILE * (c + 1)] = system_tile(
            gram, born, mass, k, c
        )
    for k in range(4):
        rows = slice(TILE * k, TILE * (k + 1))
        first = TILE * k
        if k > 0:
            a_ref[rows, first:] = a_ref[rows, first:] - jnp.dot(
                out_ref[rows, :first],
                a_ref[:first, first:],
                precision=lax.Precision.HIGHEST,
                preferred_element_type=F32,
            )
            out_ref[:first, rows] = jnp.zeros((first, TILE), F32)
            factor_panel(a_ref.at[rows, first:], 4 - k)
        for c in range(k, 4):
            out_ref[TILE * c : TILE * (c + 1), rows] = a_ref[rows, TILE * c : TILE * (c + 1)].T


def local(elem_rows, elem_block, send_lists, halo_block, born_rows, born_owner, mass):
    rows = elem_rows.shape[0]
    listed = send_lists.shape[0] // 2
    dom_size, rep_size = lax.axis_size("dom"), lax.axis_size("rep")
    rep = lax.axis_index("rep").astype(jnp.int32).reshape(1)
    shape = jax.ShapeDtypeStruct
    lists = send_lists.reshape(1, -1)
    narrow = shape((W, listed), BF16)
    cols, to_lower, to_upper = call(
        listed_kernel,
        (shape((W, rows), BF16), narrow, narrow),
        4 * W * rows * listed + 2 * W * W * rows,
        elem_rows,
        lists,
        anywhere=(0,),
        out_space=pltpu.HBM,
        vmem=VMEM_WHOLE,
        scratch=(
            pltpu.VMEM((rows, W), BF16),
            pltpu.VMEM((W, rows), BF16),
            pltpu.VMEM((W, listed), BF16),
            pltpu.VMEM((W, listed), BF16),
            pltpu.SemaphoreType.DMA((4,)),
            pltpu.SemaphoreType.DMA((12,)),
        ),
        name="listed",
    )
    up = [(i, i + 1) for i in range(dom_size - 1)]
    down = [(j, i) for i, j in up]
    from_lower = lax.ppermute(to_upper, "dom", up)
    from_upper = lax.ppermute(to_lower, "dom", down)

    slots = dom_size * rep_size
    packed = call(
        pack_kernel,
        shape((slots, CAP, W), BF16),
        2 * slots * CAP * W * W,
        born_owner.reshape(1, -1),
        born_rows,
        anywhere=(1,),
        scratch=(pltpu.VMEM(born_rows.shape, BF16), pltpu.SemaphoreType.DMA),
        vmem=VMEM_MOST,
        name="pack_born",
    )
    arrived = lax.all_to_all(packed, ("dom", "rep"), split_axis=0, concat_axis=0, tiled=True)
    born_gram = call(
        born_gram_kernel, shape((W, W), F32), 2 * slots * CAP * W * W, arrived, name="born_gram"
    )

    mixed, plain = shape((2 * MIXED, TILE), F32), shape((2 * PLAIN, TILE), F32)
    halves = {1: (mixed, plain), 2: (plain, mixed)}

    def gram(kept, parts, after, name):
        return call(
            functools.partial(gram_kernel, kept, parts),
            tuple(half for part in parts for half in halves[part]),
            3 * 6 * 2 * TILE * 256 * (rows + 2 * listed) * len(parts),
            rep,
            cols,
            from_lower,
            from_upper,
            elem_block.reshape(1, -1),
            halo_block.reshape(1, -1),
            after,
            smem=(0,),
            anywhere=(6,),
            name=name,
        )

    pair = [(i, i ^ 1) for i in range(rep_size)]
    mirror = [(i, 3 - i) for i in range(rep_size)]
    come, after = {}, packed
    for part, name in ((1, "sent_gram_1"), (2, "sent_gram_2")):
        a, b = gram(False, (part,), after, name)
        after = a
        come[part] = lax.ppermute(a, "rep", pair), lax.ppermute(b, "rep", mirror)
    ka1, kb1, ka2, kb2 = gram(True, (1, 2), after, "kept_gram")
    pieces = {}
    after = ka2
    for part, ka, kb in ((1, ka1, kb1), (2, ka2, kb2)):
        ra, rb = come[part]
        a_size, b_size = ka.shape[0] // 2, kb.shape[0] // 2
        a_next, b_next = call(
            onward_kernel,
            (shape((a_size, TILE), F32), shape((b_size, TILE), F32)),
            10**6,
            ka,
            ra,
            kb,
            rb,
            after,
            anywhere=(4,),
            name=f"onward_{part}",
        )
        after = a_next
        a2 = lax.ppermute(a_next, "rep", mirror)
        b2 = lax.ppermute(b_next, "rep", pair)
        pieces[part] = ka, ra, a2, kb, rb, b2
    mass_row = mass.reshape(1, -1)
    top, following = call(
        first_panel_kernel,
        (shape((TILE, W), F32), shape((TILE, TILE), F32)),
        10**9,
        *pieces[1],
        born_gram,
        mass_row,
        name="first_panel",
    )
    return call(
        other_panels_kernel,
        shape((W, W), F32),
        2 * 10**9,
        *pieces[2],
        born_gram,
        mass_row,
        top,
        following,
        scratch=(pltpu.VMEM((W, W), F32),),
        name="other_panels",
    )


def solution(mesh):
    in_specs = (
        P(("dom", "rep"), None),
        P(("dom", "rep")),
        P(("dom", "rep")),
        P(("dom", "rep")),
        P(("dom", "rep"), None),
        P(("dom", "rep"), None),
        P(("dom", "rep")),
    )
    out_specs = P(("dom", "rep"), None)
    return jax.shard_map(local, mesh=mesh, in_specs=in_specs, out_specs=out_specs, check_vma=False)
```

```python
import functools

import jax
import jax.numpy as jnp
from jax import lax
from jax.experimental import pallas as pl
from jax.experimental.pallas import tpu as pltpu
from jax.sharding import PartitionSpec as P

CAP = 4
W = 512
TILE = 128
F32 = jnp.float32
BF16 = jnp.bfloat16
VMEM_LIMIT = 24 * 1024 * 1024
VMEM_WHOLE = 63 * 1024 * 1024 + 512 * 1024
NT_DIMS = (((1,), (1,)), ((), ()))
PLAIN = 2 * TILE
MIXED = 2 * TILE + 8


def call(kernel, outs, flops, *args, smem=(), anywhere=(), out_space=pltpu.VMEM, scratch=(), vmem=VMEM_LIMIT, name=None):
    specs = [
        pl.BlockSpec(
            memory_space=pltpu.SMEM if i in smem else pltpu.HBM if i in anywhere else pltpu.VMEM
        )
        for i in range(len(args))
    ]
    single = not isinstance(outs, (tuple, list))
    size = sum(a.size * a.dtype.itemsize for a in args)
    return pl.pallas_call(
        kernel,
        out_shape=outs,
        in_specs=specs,
        out_specs=pl.BlockSpec(memory_space=out_space)
        if single
        else [pl.BlockSpec(memory_space=out_space)] * len(outs),
        scratch_shapes=list(scratch),
        compiler_params=pltpu.CompilerParams(vmem_limit_bytes=vmem),
        cost_estimate=pl.CostEstimate(flops=flops, bytes_accessed=size, transcendentals=0),
        name=name,
    )(*args)


def listed_kernel(
    rows_ref, list_ref, cols_out, lower_out, upper_out, rows, cols, lower, upper, in_sems, sems
):
    total, listed = rows.shape[0], lower.shape[1]
    piece = total // in_sems.shape[0]
    copies = []
    for i in range(in_sems.shape[0]):
        part = pl.ds(i * piece, piece)
        copies.append(pltpu.make_async_copy(rows_ref.at[part, :], rows.at[part, :], in_sems.at[i]))
        copies[-1].start()
    sent = []

    def send(source, target, c, width):
        part = pl.ds(c, width)
        sent.append(
            pltpu.make_async_copy(source.at[:, part], target.at[:, part], sems.at[len(sent)])
        )
        sent[-1].start()

    for i, copy in enumerate(copies):
        copy.wait()
        c = i * piece
        cols[:, c : c + piece] = rows[c : c + piece, :].T
        send(cols, cols_out, c, piece)
    step, deep = 256, 256
    places = lax.broadcasted_iota(jnp.int32, (deep, step), 0).astype(BF16)
    for buf, target, first in ((upper, upper_out, listed), (lower, lower_out, 0)):
        for c in range(0, listed, step):
            names = list_ref[:, first + c : first + c + step]
            hot = []
            for h in range(0, total, deep):
                near = jnp.clip(names - h, -1, deep).astype(F32).astype(BF16)
                hot.append(jnp.maximum(1 - jnp.abs(places - near), 0).astype(BF16))
            buf[:, c : c + step] = jnp.dot(
                cols[...], jnp.concatenate(hot, axis=0), preferred_element_type=F32
            ).astype(BF16)
            send(buf, target, c, step)
    for copy in sent:
        copy.wait()


def pack_kernel(owner_ref, rows_ref, out_ref):
    owner = owner_ref[...]
    count = owner.shape[1]
    blocks = out_ref.shape[0]
    named = lax.broadcasted_iota(jnp.int32, (blocks, count), 0) == owner
    named = jnp.where(named, 1.0, 0.0)
    before = lax.broadcasted_iota(jnp.int32, (count, count), 0) < lax.broadcasted_iota(
        jnp.int32, (count, count), 1
    )
    before = jnp.where(before, 1.0, 0.0).astype(BF16)
    earlier = jnp.dot(named.astype(BF16), before, preferred_element_type=F32)
    rank = jnp.sum(named * earlier, axis=0, keepdims=True)
    place = owner * CAP + rank.astype(jnp.int32)
    deep = 256
    slots = lax.broadcasted_iota(jnp.int32, (deep, count), 0).astype(BF16)
    hot = []
    for h in range(0, blocks * CAP, deep):
        near = jnp.clip(place - h, -1, deep).astype(F32).astype(BF16)
        hot.append(jnp.maximum(1 - jnp.abs(slots - near), 0).astype(BF16))
    hot = jnp.concatenate(hot, axis=0)
    packed = jnp.dot(hot, rows_ref[...], preferred_element_type=F32).astype(BF16)
    out_ref[...] = packed.reshape(out_ref.shape)


LEFT = {1: ((0, "a"), (1, "a")), 2: ()}
RIGHT = {1: ((0, "b"),), 2: ((1, "a"), (2, "b"), (3, "b"))}


def place_pair(out_ref, at, first, second, between):
    sub = lax.broadcasted_iota(jnp.int32, (TILE, TILE), 0)
    lane = lax.broadcasted_iota(jnp.int32, (TILE, TILE), 1)
    out_ref[at : at + TILE, :] = jnp.where(lane >= sub, first, second)
    out_ref[at + TILE : at + 2 * TILE, :] = between
    diagonal = jnp.sum(jnp.where(lane == sub, second, 0.0), axis=0, keepdims=True)
    out_ref[at + 2 * TILE : at + MIXED, :] = jnp.broadcast_to(diagonal, (8, TILE))


def gram_kernel(kept, parts, rep_ref, cols, lo, up, ids, halo_ids, after, *outs):
    me = rep_ref[0]
    pair, mirror, far = me ^ 1, 3 - me, me ^ 2
    blocks = {
        "a": (me, mirror) if kept else (pair, far),
        "b": (me, pair) if kept else (mirror, far),
    }
    half, own = lo.shape[1], cols.shape[1]
    pieces = [(cols, ids, c) for c in range(0, own, 1024)]
    pieces += [(lo, halo_ids.at[:, :half], 0), (up, halo_ids.at[:, half:], 0)]
    left_rows = [r for part in parts for r in LEFT[part]]
    right_rows = [r for part in parts for r in RIGHT[part]]
    left = right = None
    for buf, names_ref, c in pieces:
        span = slice(c, c + 1024)
        names = names_ref[:, span]
        masks = {
            k: [jnp.where(names == block, 1.0, 0.0).astype(BF16) for block in v]
            for k, v in blocks.items()
        }
        part = {}
        for panel, k in dict.fromkeys(left_rows + right_rows):
            x = buf[panel * TILE : (panel + 1) * TILE, span]
            part[panel, k] = [x * m for m in masks[k]]

        def product(rows, columns):
            stack = jnp.concatenate([x for r in rows for x in part[r]], axis=0)
            return lax.dot_general(
                stack, buf[columns, span], NT_DIMS, preferred_element_type=F32
            )

        r = product(right_rows, slice(256, 512))
        right = r if right is None else right + r
        if left_rows:
            l = product(left_rows, slice(0, 256))
            left = l if left is None else left + l

    def tiles(value, rows, which, i):
        at = (2 * rows.index(which) + i) * TILE
        return value[at : at + TILE, :TILE], value[at : at + TILE, TILE:]

    for part, a_ref, b_ref in zip(parts, outs[::2], outs[1::2]):
        for i in range(2):
            if part == 1:
                first, between = tiles(left, left_rows, (0, "a"), i)
                _, second = tiles(left, left_rows, (1, "a"), i)
                place_pair(a_ref, i * MIXED, first, second, between)
                plain_ref, plain = b_ref, tiles(right, right_rows, (0, "b"), i)
            else:
                first, between = tiles(right, right_rows, (2, "b"), i)
                _, second = tiles(right, right_rows, (3, "b"), i)
                place_pair(b_ref, i * MIXED, first, second, between)
                plain_ref, plain = a_ref, tiles(right, right_rows, (1, "a"), i)
            for j in range(2):
                at = i * PLAIN + j * TILE
                plain_ref[at : at + TILE, :] = plain[j]


def born_gram_kernel(pool_ref, out_ref):
    pool = pool_ref[...].reshape(-1, W)
    dims = (((0,), (0,)), ((), ()))
    out_ref[...] = lax.dot_general(pool, pool, dims, preferred_element_type=F32)


def lane_copy(x, c):
    return jnp.broadcast_to(x[:, c : c + 1], (8, TILE))


def row_copy(x, i):
    return jnp.broadcast_to(x[i : i + 1, :], (8, TILE))


def add_all(xs):
    while len(xs) > 1:
        xs = [xs[i] + xs[i + 1] if i + 1 < len(xs) else xs[i] for i in range(0, len(xs), 2)]
    return xs[0]


def inverse_factor(columns):
    a = [[row_copy(columns[j], i) if i >= j else None for j in range(8)] for i in range(8)]
    low = [[None] * 8 for _ in range(8)]
    pivots = []
    for b in range(0, 8, 2):
        p, q, r = a[b][b], a[b + 1][b], a[b + 1][b + 1]
        det = p * r - q * q
        root, root_det = lax.rsqrt(p), lax.rsqrt(det)
        both = root * root_det
        pivots.append((root, -(q * both), p * both))
        for i in range(b + 2, 8):
            x, y = a[i][b], a[i][b + 1]
            low[i][b] = x * root
            low[i][b + 1] = (y * p - x * q) * both
        for i in range(b + 2, 8):
            for k in range(b + 2, i + 1):
                a[i][k] = a[i][k] - low[i][b] * low[k][b] - low[i][b + 1] * low[k][b + 1]
    inv = [[None] * 8 for _ in range(8)]
    for b in range(0, 8, 2):
        i0, i1, i2 = pivots[b // 2]
        inv[b][b], inv[b + 1][b], inv[b + 1][b + 1] = i0, i1, i2
        for m in range(b):
            s0 = add_all([low[b][k] * inv[k][m] for k in range(m, b)])
            s1 = add_all([low[b + 1][k] * inv[k][m] for k in range(m, b)])
            inv[b][m] = -(i0 * s0)
            inv[b + 1][m] = -(i1 * s0 + i2 * s1)
    return inv


SUB = 64


def factor_panel(a_ref, tiles):
    sub = lax.broadcasted_iota(jnp.int32, (8, TILE), 0)
    lane = lax.broadcasted_iota(jnp.int32, (8, TILE), 1)
    cols = [slice(TILE * c, TILE * c + TILE) for c in range(tiles)]
    pivot = None
    for s in range(16):
        o = 8 * s
        last = (o // SUB + 1) * SUB // 8
        if pivot is None:
            head = a_ref[o : o + 8, cols[0]]
            pivot = [lane_copy(head, o + j) for j in range(8)]
        inv = inverse_factor(pivot)
        pivot = near = None
        if s + 1 < last:
            head = a_ref[o + 8 : o + 16, cols[0]]
            b = [lane_copy(head, o + m) for m in range(8)]
            own = [lane_copy(head, o + 8 + j) for j in range(8)]
            near = [add_all([inv[j][m] * b[m] for m in range(j + 1)]) for j in range(8)]
            pivot = [
                own[j] - add_all([near[m] * row_copy(near[m], j) for m in range(8)])
                for j in range(8)
            ]
        columns = []
        for m in range(8):
            v = inv[7][m]
            for i in range(6, m - 1, -1):
                v = jnp.where(sub <= i, inv[i][m], v)
            if m > 0:
                v = jnp.where(sub < m, 0.0, v)
            columns.append(v)
        upper = []
        for c in cols:
            x = a_ref[o : o + 8, c]
            upper.append(add_all([columns[m] * row_copy(x, m) for m in range(8)]))
        upper[0] = jnp.where(lane >= sub + o, upper[0], 0.0)
        for u, c in zip(upper, cols):
            a_ref[o : o + 8, c] = u
        if s + 1 < last:
            spread = [[row_copy(u, j) for j in range(8)] for u in upper]
            for g in range(s + 1, last):
                rows = slice(8 * g, 8 * g + 8)
                x = a_ref[rows, cols[0]]
                low = near
                if g > s + 1:
                    b = [lane_copy(x, o + m) for m in range(8)]
                    low = [add_all([inv[j][m] * b[m] for m in range(j + 1)]) for j in range(8)]
                for i, c in enumerate(cols):
                    y = x if i == 0 else a_ref[rows, c]
                    a_ref[rows, c] = y - add_all([low[j] * spread[i][j] for j in range(8)])
        elif s + 1 < 16:
            done = a_ref[o + 8 - SUB : o + 8, :]
            a_ref[o + 8 : TILE, :] = a_ref[o + 8 : TILE, :] - lax.dot_general(
                done[:, o + 8 : TILE],
                done,
                (((0,), (0,)), ((), ())),
                precision=lax.Precision.HIGHEST,
                preferred_element_type=F32,
            )


def onward_kernel(ka, ra, kb, rb, after, a_ref, b_ref):
    a_size, b_size = a_ref.shape[0], b_ref.shape[0]
    a_ref[...] = ka[a_size:, :] + ra[a_size:, :]
    b_ref[...] = kb[b_size:, :] + rb[b_size:, :]


def tile_sum(kept, come, last, at):
    span = slice(at, at + TILE)
    return kept[span, :] + come[span, :] + last[span, :]


def split_pair(kept, come, last):
    sub = lax.broadcasted_iota(jnp.int32, (TILE, TILE), 0)
    lane = lax.broadcasted_iota(jnp.int32, (TILE, TILE), 1)
    both = tile_sum(kept, come, last, 0)
    flip = both.T
    row = slice(2 * TILE, 2 * TILE + 1)
    diagonal = kept[row, :] + come[row, :] + last[row, :]
    second = jnp.where(lane < sub, both, jnp.where(lane == sub, diagonal, flip))
    return jnp.where(lane >= sub, both, flip), second


def system_tile(gram, born, mass, k, c):
    rows, cols = slice(TILE * k, TILE * (k + 1)), slice(TILE * c, TILE * (c + 1))
    value = (gram + born[rows, cols]) * (1.0 / W)
    if k == c:
        sub = lax.broadcasted_iota(jnp.int32, (TILE, TILE), 0)
        lane = lax.broadcasted_iota(jnp.int32, (TILE, TILE), 1)
        value = value + jnp.where(sub == lane, mass[:, rows], 0.0)
    return value


def first_panel_kernel(ka, ra, a2, kb, rb, b2, born, mass, top_ref, next_ref):
    first, second = split_pair(ka, ra, a2)
    top = [first, tile_sum(ka, ra, a2, TILE), tile_sum(kb, rb, b2, 0), tile_sum(kb, rb, b2, TILE)]
    for c in range(4):
        top_ref[:, TILE * c : TILE * (c + 1)] = system_tile(top[c], born, mass, 0, c)
    next_ref[...] = system_tile(second, born, mass, 1, 1)
    factor_panel(top_ref, 4)


def other_panels_kernel(ka, ra, a2, kb, rb, b2, born, mass, top_ref, next_ref, out_ref, a_ref):
    third, fourth = split_pair(kb, rb, b2)
    grams = {
        (1, 2): tile_sum(ka, ra, a2, 0),
        (1, 3): tile_sum(ka, ra, a2, TILE),
        (2, 2): third,
        (2, 3): tile_sum(kb, rb, b2, TILE),
        (3, 3): fourth,
    }
    a_ref[:TILE, :] = top_ref[...]
    a_ref[TILE : 2 * TILE, TILE : 2 * TILE] = next_ref[...]
    for (k, c), gram in grams.items():
        a_ref[TILE * k : TILE * (k + 1), TILE * c : TILE * (c + 1)] = system_tile(
            gram, born, mass, k, c
        )
    for k in range(4):
        rows = slice(TILE * k, TILE * (k + 1))
        first = TILE * k
        if k > 0:
            a_ref[rows, first:] = a_ref[rows, first:] - jnp.dot(
                out_ref[rows, :first],
                a_ref[:first, first:],
                precision=lax.Precision.HIGHEST,
                preferred_element_type=F32,
            )
            out_ref[:first, rows] = jnp.zeros((first, TILE), F32)
            factor_panel(a_ref.at[rows, first:], 4 - k)
        for c in range(k, 4):
            out_ref[TILE * c : TILE * (c + 1), rows] = a_ref[rows, TILE * c : TILE * (c + 1)].T


def local(elem_rows, elem_block, send_lists, halo_block, born_rows, born_owner, mass):
    rows = elem_rows.shape[0]
    listed = send_lists.shape[0] // 2
    dom_size, rep_size = lax.axis_size("dom"), lax.axis_size("rep")
    rep = lax.axis_index("rep").astype(jnp.int32).reshape(1)
    shape = jax.ShapeDtypeStruct
    lists = send_lists.reshape(1, -1)
    narrow = shape((W, listed), BF16)
    cols, to_lower, to_upper = call(
        listed_kernel,
        (shape((W, rows), BF16), narrow, narrow),
        4 * W * rows * listed + 2 * W * W * rows,
        elem_rows,
        lists,
        anywhere=(0,),
        out_space=pltpu.HBM,
        vmem=VMEM_WHOLE,
        scratch=(
            pltpu.VMEM((rows, W), BF16),
            pltpu.VMEM((W, rows), BF16),
            pltpu.VMEM((W, listed), BF16),
            pltpu.VMEM((W, listed), BF16),
            pltpu.SemaphoreType.DMA((4,)),
            pltpu.SemaphoreType.DMA((12,)),
        ),
        name="listed",
    )
    up = [(i, i + 1) for i in range(dom_size - 1)]
    down = [(j, i) for i, j in up]
    from_lower = lax.ppermute(to_upper, "dom", up)
    from_upper = lax.ppermute(to_lower, "dom", down)

    slots = dom_size * rep_size
    packed = call(
        pack_kernel,
        shape((slots, CAP, W), BF16),
        2 * slots * CAP * W * W,
        born_owner.reshape(1, -1),
        born_rows,
        name="pack_born",
    )
    arrived = lax.all_to_all(packed, ("dom", "rep"), split_axis=0, concat_axis=0, tiled=True)
    born_gram = call(
        born_gram_kernel, shape((W, W), F32), 2 * slots * CAP * W * W, arrived, name="born_gram"
    )

    mixed, plain = shape((2 * MIXED, TILE), F32), shape((2 * PLAIN, TILE), F32)
    halves = {1: (mixed, plain), 2: (plain, mixed)}

    def gram(kept, parts, after, name):
        return call(
            functools.partial(gram_kernel, kept, parts),
            tuple(half for part in parts for half in halves[part]),
            3 * 6 * 2 * TILE * 256 * (rows + 2 * listed) * len(parts),
            rep,
            cols,
            from_lower,
            from_upper,
            elem_block.reshape(1, -1),
            halo_block.reshape(1, -1),
            after,
            smem=(0,),
            anywhere=(6,),
            name=name,
        )

    pair = [(i, i ^ 1) for i in range(rep_size)]
    mirror = [(i, 3 - i) for i in range(rep_size)]
    come, after = {}, packed
    for part, name in ((1, "sent_gram_1"), (2, "sent_gram_2")):
        a, b = gram(False, (part,), after, name)
        after = a
        come[part] = lax.ppermute(a, "rep", pair), lax.ppermute(b, "rep", mirror)
    ka1, kb1, ka2, kb2 = gram(True, (1, 2), after, "kept_gram")
    pieces = {}
    after = ka2
    for part, ka, kb in ((1, ka1, kb1), (2, ka2, kb2)):
        ra, rb = come[part]
        a_size, b_size = ka.shape[0] // 2, kb.shape[0] // 2
        a_next, b_next = call(
            onward_kernel,
            (shape((a_size, TILE), F32), shape((b_size, TILE), F32)),
            10**6,
            ka,
            ra,
            kb,
            rb,
            after,
            anywhere=(4,),
            name=f"onward_{part}",
        )
        after = a_next
        a2 = lax.ppermute(a_next, "rep", mirror)
        b2 = lax.ppermute(b_next, "rep", pair)
        pieces[part] = ka, ra, a2, kb, rb, b2
    mass_row = mass.reshape(1, -1)
    top, following = call(
        first_panel_kernel,
        (shape((TILE, W), F32), shape((TILE, TILE), F32)),
        10**9,
        *pieces[1],
        born_gram,
        mass_row,
        name="first_panel",
    )
    return call(
        other_panels_kernel,
        shape((W, W), F32),
        2 * 10**9,
        *pieces[2],
        born_gram,
        mass_row,
        top,
        following,
        scratch=(pltpu.VMEM((W, W), F32),),
        name="other_panels",
    )


def solution(mesh):
    in_specs = (
        P(("dom", "rep"), None),
        P(("dom", "rep")),
        P(("dom", "rep")),
        P(("dom", "rep")),
        P(("dom", "rep"), None),
        P(("dom", "rep"), None),
        P(("dom", "rep")),
    )
    out_specs = P(("dom", "rep"), None)
    return jax.shard_map(local, mesh=mesh, in_specs=in_specs, out_specs=out_specs, check_vma=False)
```
